32 devices in a mesh: dp: 16 (over z, x, core), tensor: 2 (over y).
Axes of the slice: x: 2, y: 2, z: 4, core: 2. Of those that a mesh axis runs over, the one named last changes fastest.
Arguments:
- tokens_in: bfloat16 [24576, 768], P(('dp', 'tensor')), may hold values from -6 to 6
- seq_lengths: int32 [16, 3], P('dp'), may hold values from 1 to 1024, 1536 in all within a row
- norm1_gain: float32 [768], replicated, may hold values from 0.5 to 1.5
- norm2_gain: float32 [768], replicated, may hold values from 0.5 to 1.5
- w_qkv: bfloat16 [3, 768, 768], P(None, None, 'tensor'), may hold values from -0.21875 to 0.21875
- w_out: bfloat16 [768, 768], P('tensor'), may hold values from -0.625 to 0.625
- w_in: bfloat16 [2, 768, 1152], P(None, None, 'tensor'), may hold values from -0.21875 to 0.21875
- w_down: bfloat16 [1152, 768], P('tensor'), may hold values from -0.1875 to 0.1875
- out_grad: bfloat16 [24576, 768], P(('dp', 'tensor')), may hold values from -6 to 6
Outputs:
- out_tokens: bfloat16 [24576, 768], P(('dp', 'tensor'))
- in_grad: bfloat16 [24576, 768], P(('dp', 'tensor'))
- grad_norm1: float32 [768], replicated
- grad_norm2: float32 [768], replicated
- grad_qkv: float32 [3, 768, 768], P(None, None, 'tensor')
- grad_out: float32 [768, 768], P('tensor')
- grad_in: float32 [2, 768, 1152], P(None, None, 'tensor')
- grad_down: float32 [1152, 768], P('tensor')
The draws below stay inside these ranges and needn't reach their ends.
Inputs may be any that keep to these rules, and one draw needn't show every extreme that they name: Each row of seq_lengths gives the lengths of the 3 sequences of one group in order; they sum to 1536, and the longest of each row is exactly 1024.
All inputs are finite; a program needn't handle non-finite values.
Results may differ from the reference program's by a relative error of at most 0.02.
Values may be sent and summed in bfloat16 or wider, within the bound.
No kernel may reach another device: no remote copies, remote signals or barrier semaphores. Data moves between devices by JAX's collectives and lax.ppermute only.
A program may use at most 128 MiB of HBM per device.

```python
import math
import jax
import jax.numpy as jnp
import numpy as np
from jax import lax

D = 768
HEADS = 12
HEAD_DIM = 64
FF = 1152
HALF = 64
BLOCK = 512
PIECES = 3
TOK_DEV = 1536
LONGEST = 1024
GROUPS = 16
TOKENS = 24576


def levels(own_key, dims, shards, low, top_value):
    level, own = 1.0, jax.random.fold_in(own_key, 6)
    for dim, shards_of in shards:
        draws = jnp.exp(jax.random.uniform(jax.random.fold_in(own, dim), (shards_of,), jnp.float32, low / len(shards), top_value / len(shards)))
        level = level * jnp.repeat(draws, dims[dim] // shards_of).reshape([-1 if axis == dim else 1 for axis in range(len(dims))])
    return level


def profile(count, total, most, skew):
    loads = [(1 << 20) // math.isqrt(rank ** skew) + 1 for rank in range(2, count + 1)]
    rest, given = total - most - (count - 1), [1] * (count - 1)
    while rest > 0:
        candidates = [i for i in range(count - 1) if given[i] < most]
        whole, remaining = sum([loads[i] for i in candidates]), rest
        for i in candidates:
            extra = min(most - given[i], max(1, remaining * loads[i] // whole), rest)
            given[i] = given[i] + extra
            rest = rest - extra
    return np.array([most] + given)


def uneven(stream_key, amount, total, bound, skew):
    if amount == 2:
        one = jax.random.randint(stream_key, (), max(1, total - bound), min(bound, total - 1) + 1)
        return jnp.stack([one, total - one])
    sizes = jnp.asarray(profile(amount, total, bound, skew), jnp.int32)
    twos = (amount - 1) // 2
    donor, taker = sizes[1:1 + 2 * twos:2], sizes[2:2 + 2 * twos:2]
    margin = jnp.minimum(donor - 1, bound - taker)
    shifted = jax.random.randint(jax.random.fold_in(stream_key, 1), (twos,), 0, 1 << 20) % (margin + 1)
    sizes = sizes.at[1:1 + 2 * twos:2].set(donor - shifted).at[2:2 + 2 * twos:2].set(taker + shifted)
    return sizes[jax.random.permutation(jax.random.fold_in(stream_key, 2), amount)]


def scatter_about(key, dims, width, most, cuts=(), kind=jnp.bfloat16):
    loudness = levels(key, dims, cuts, -0.22, 0.18) if cuts else 1.0
    result = jax.random.normal(key, dims, jnp.float32) * width * loudness
    return jnp.minimum(jnp.maximum(result, -most), most).astype(kind)


def setup_inputs(seed: int = 0) -> dict:
    keys = jax.random.split(jax.random.key(seed), 10)
    return {
        "tokens_in": scatter_about(keys[0], (TOKENS, D), 1.0, 6.0, ((0, 32),)),
        "seq_lengths": jax.vmap(lambda own: uneven(own, PIECES, TOK_DEV, LONGEST, 1))(jax.random.split(keys[1], GROUPS)).reshape((GROUPS, PIECES)).astype(jnp.int32),
        "norm1_gain": jnp.clip(1.0 + 0.1 * jax.random.normal(keys[2], (D,), jnp.float32), 0.5, 1.5),
        "norm2_gain": jnp.clip(1.0 + 0.1 * jax.random.normal(keys[3], (D,), jnp.float32), 0.5, 1.5),
        "w_qkv": scatter_about(keys[4], (3, D, D), D ** -0.5, 0.21875, ((2, 2),)),
        "w_out": scatter_about(keys[5], (D, D), (D // 8) ** -0.5, 0.625, ((0, 2),)),
        "w_in": scatter_about(keys[6], (2, D, FF), D ** -0.5, 0.21875, ((2, 2),)),
        "w_down": scatter_about(keys[7], (FF, D), FF ** -0.5, 0.1875, ((0, 2),)),
        "out_grad": scatter_about(keys[8], (TOKENS, D), 1.0, 6.0, ((0, 32),)),
    }


precise = lax.Precision.HIGHEST

@jax.custom_vjp
def low(v):
    return lax.optimization_barrier(v.astype(jnp.bfloat16)).astype(jnp.float32)

@jax.custom_vjp
def low_back(v):
    return v

def low_keep(v):
    return (low(v), None)

def low_pass(kept, grad):
    return (grad,)

def back_keep(v):
    return (v, None)

def back_low(kept, grad):
    return (low(grad),)
low.defvjp(low_keep, low_pass)
low_back.defvjp(back_keep, back_low)

def places(lengths, group_rows):
    indices = jnp.arange(group_rows, dtype=jnp.int32)
    ends = jnp.cumsum(lengths).astype(jnp.int32)
    passed_end = indices[:, None] >= ends[None, :]
    segment = lax.optimization_barrier(jnp.sum(passed_end.astype(jnp.int32), axis=1)).astype(jnp.int32)
    opening = lax.optimization_barrier(jnp.sum(jnp.where(passed_end, lengths[None, :], 0), axis=1)).astype(jnp.int32)
    return (segment, (indices - opening).astype(jnp.int32))

def rotations(position):
    frequency = 10000.0 ** (-jnp.arange(0, HEAD_DIM, 2, dtype=jnp.float32) / HEAD_DIM)
    angle_all = position.astype(jnp.float32)[:, None] * frequency[None, :]
    angle_all = jnp.concatenate([angle_all, angle_all], axis=1)[:, None, :]
    return (jnp.cos(angle_all), jnp.sin(angle_all))

def turn_half(values):
    half_dim = values.shape[-1] // 2
    return jnp.concatenate([-values[..., half_dim:], values[..., :half_dim]], axis=-1)

def rotate(values, cosine, sine_part):
    return values * cosine + turn_half(values) * sine_part

def layer_norm(values, gain_vec):
    centred = values - lax.optimization_barrier(jnp.mean(values, axis=-1, keepdims=True))
    spread = lax.optimization_barrier(jnp.mean(centred * centred, axis=-1, keepdims=True))
    return centred * lax.rsqrt(spread + 1e-05) * gain_vec

def window_mask(segment, offset):
    padded_seg = jnp.pad(segment, (HALF, HALF), constant_values=-1)
    query_seg = lax.dynamic_slice_in_dim(segment, offset, BLOCK)
    key_seg = lax.dynamic_slice_in_dim(padded_seg, offset, BLOCK + 2 * HALF)
    query_idx = offset + jnp.arange(BLOCK, dtype=jnp.int32)
    key_idx = offset - HALF + jnp.arange(BLOCK + 2 * HALF, dtype=jnp.int32)
    return (query_seg[:, None] == key_seg[None, :]) & (jnp.abs(query_idx[:, None] - key_idx[None, :]) <= HALF)

def attention(queries, keys_all, values_all, segment):
    group_rows = queries.shape[0]
    keys_pad = jnp.pad(keys_all, ((HALF, HALF), (0, 0), (0, 0)))
    values_pad = jnp.pad(values_all, ((HALF, HALF), (0, 0), (0, 0)))
    score_scale = HEAD_DIM ** (-0.5)

    @jax.checkpoint
    def one_block(offset):
        q_block = lax.dynamic_slice_in_dim(queries, offset, BLOCK, 0)
        k_block = lax.dynamic_slice_in_dim(keys_pad, offset, BLOCK + 2 * HALF, 0)
        v_block = lax.dynamic_slice_in_dim(values_pad, offset, BLOCK + 2 * HALF, 0)
        allowed = window_mask(segment, offset)
        scores = low_back(score_scale * jnp.einsum('qhd,khd->hqk', q_block, k_block, precision=precise))
        scores = jnp.where(allowed[None], scores, -1e+30)
        peak_score = lax.optimization_barrier(jnp.max(scores, axis=-1, keepdims=True))
        raw_weights = jnp.exp(scores - peak_score)
        probability = raw_weights / lax.optimization_barrier(jnp.sum(raw_weights, axis=-1, keepdims=True))
        mixed_rows = jnp.einsum('hqk,khd->qhd', low(probability), v_block, precision=precise)
        return mixed_rows.reshape(BLOCK, -1)
    offsets = jnp.arange(group_rows // BLOCK, dtype=jnp.int32) * BLOCK
    return lax.map(one_block, offsets).reshape(group_rows, -1)

def forward(tokens, gain_one, gain_two, w_qkv, w_out, w_in, w_down, segment, cosine, sine_part):
    group_rows = tokens.shape[0]
    head_shape = (group_rows, HEADS, HEAD_DIM)
    norm_one = low(layer_norm(tokens, gain_one))
    raw_query = low_back(jnp.dot(norm_one, w_qkv[0], precision=precise)).reshape(head_shape)
    raw_key = low_back(jnp.dot(norm_one, w_qkv[1], precision=precise)).reshape(head_shape)
    raw_value = low_back(jnp.dot(norm_one, w_qkv[2], precision=precise)).reshape(head_shape)
    queries = low(rotate(raw_query, cosine, sine_part))
    keys_all = low(rotate(raw_key, cosine, sine_part))
    values_all = low(raw_value)
    mixed_rows = low(low_back(attention(queries, keys_all, values_all, segment)))
    residual = tokens + low_back(jnp.dot(mixed_rows, w_out, precision=precise))
    norm_two = low(layer_norm(residual, gain_two))
    up_in = low_back(jnp.dot(norm_two, w_in[0], precision=precise))
    gate_vals = low_back(jnp.dot(norm_two, w_in[1], precision=precise))
    act_rows = low(jax.nn.gelu(up_in, approximate=False) * gate_vals)
    return residual + low_back(jnp.dot(act_rows, w_down, precision=precise))

def reference(tokens_in, seq_lengths, norm1_gain, norm2_gain, w_qkv, w_out, w_in, w_down, out_grad):
    params = (norm1_gain.astype(jnp.float32), norm2_gain.astype(jnp.float32), w_qkv.astype(jnp.float32), w_out.astype(jnp.float32), w_in.astype(jnp.float32), w_down.astype(jnp.float32))
    tokens_grp = tokens_in.astype(jnp.float32).reshape(GROUPS, TOK_DEV, D)
    grads_grp = out_grad.astype(jnp.float32).reshape(GROUPS, TOK_DEV, D)

    def group_step(totals, block_item):
        tokens, d_output, lengths = block_item
        segment, position = places(lengths, TOK_DEV)
        cosine, sine_part = rotations(position)

        def layer(tokens_arg, gain_one, gain_two, weight_qkv, weight_out, weight_in, weight_down):
            return forward(tokens_arg, gain_one, gain_two, weight_qkv, weight_out, weight_in, weight_down, segment, cosine, sine_part)
        output, pullback = jax.vjp(layer, tokens, params[0], params[1], params[2], params[3], params[4], params[5])
        gradients = pullback(d_output)
        totals = jax.tree.map(jnp.add, totals, tuple(gradients[1:]))
        return (totals, (output.astype(jnp.bfloat16), gradients[0].astype(jnp.bfloat16)))
    initial = jax.tree.map(jnp.zeros_like, params)
    totals, (outputs, in_grads) = lax.scan(group_step, initial, (tokens_grp, grads_grp, seq_lengths))
    return (outputs.reshape(TOKENS, D), in_grads.reshape(TOKENS, D), totals[0], totals[1], totals[2], totals[3], totals[4], totals[5])
```

```python
import functools

import jax
import jax.numpy as jnp
from jax import lax
from jax.experimental import pallas as pl
from jax.experimental.pallas import tpu as pltpu
from jax.sharding import Mesh, PartitionSpec as P

HEAD_DIM = 64
HALF = 64
QB = 128
WIN = QB + 2 * HALF
SWAP = [(0, 1), (1, 0)]
BF = jnp.bfloat16
F32 = jnp.float32


def vmem(megabytes):
    return pltpu.CompilerParams(vmem_limit_bytes=megabytes * 1024 * 1024)


def spread_tables(rows, index, lengths):
    ends = jnp.cumsum(lengths)
    passed = index[:, None] >= ends[None, :]
    opening = jnp.sum(jnp.where(passed, lengths[None, :], 0), axis=1)
    position = (index - opening).astype(F32)
    frequency = 10000.0 ** (-jnp.arange(0, HEAD_DIM, 2, dtype=F32) / HEAD_DIM)
    angle = position[:, None] * frequency[None, :]
    cosine, sine = jnp.cos(angle), jnp.sin(angle)
    return (
        jnp.concatenate([cosine] * 4, axis=1),
        jnp.concatenate([-sine, sine, -sine, sine], axis=1),
    )


def normalize(values):
    centred = values - jnp.mean(values, axis=-1, keepdims=True)
    factor = lax.rsqrt(jnp.mean(centred * centred, axis=-1, keepdims=True) + 1e-05)
    return (centred * factor, factor)


def norm_back(d_norm, gain_vec, normed, factor):
    scaled = d_norm * gain_vec
    return factor * (
        scaled
        - jnp.mean(scaled, axis=-1, keepdims=True)
        - normed * jnp.mean(scaled * normed, axis=-1, keepdims=True)
    )


def partner_lanes(values):
    lane = lax.broadcasted_iota(jnp.int32, values.shape, 1)
    lower = (lane & 32) == 0
    width = values.shape[1]
    return jnp.where(
        lower, pltpu.roll(values, width - 32, 1), pltpu.roll(values, 32, 1)
    )


def window_bias(scal_ref, block, rows):
    e0, e1, t0, h0 = scal_ref[0], scal_ref[1], scal_ref[2], scal_ref[3]
    j = block * QB + lax.broadcasted_iota(jnp.int32, (WIN, QB), 0)
    t = t0 + block * QB + lax.broadcasted_iota(jnp.int32, (WIN, QB), 1)
    u = jnp.where(
        j < HALF, h0 + j, jnp.where(j >= rows + HALF, h0 + j - rows - HALF, t0 + j - HALF)
    )
    seg_t = (t >= e0).astype(jnp.int32) + (t >= e1).astype(jnp.int32)
    seg_u = (u >= e0).astype(jnp.int32) + (u >= e1).astype(jnp.int32)
    allowed = (seg_t == seg_u) & (jnp.abs(t - u) <= HALF)
    bias = jnp.where(allowed, 0.0, -1e30).astype(F32)
    return jnp.concatenate([bias, bias], axis=1)


def stack_heads(pair):
    lower = lax.broadcasted_iota(jnp.int32, pair.shape, 1) < HEAD_DIM
    zero = jnp.zeros_like(pair)
    return jnp.concatenate(
        [jnp.where(lower, pair, zero), jnp.where(lower, zero, pair)], axis=0
    )


def unstack_columns(both):
    return jnp.concatenate(
        [both[:HEAD_DIM, :QB], both[HEAD_DIM:, QB:]], axis=0
    ).T


def dot(a, b, contract):
    return lax.dot_general(a, b, ((contract[0], contract[1]), ((), ())), preferred_element_type=F32)


def qkv_attn_kernel(
    scal_ref, norm_ref, w_ref, cos_ref, sin_ref, q_ref, k_ref, v_ref, mixed_ref, lse_ref
):
    rows = q_ref.shape[0]
    ext = norm_ref.shape[0]
    width = q_ref.shape[1]
    pairs = width // 128
    step = 208 if ext % 208 == 0 else 64

    def project(i, carry):
        at = pl.ds(pl.multiple_of(i * step, 16), step)
        low = norm_ref[at, :]
        cos, sin = cos_ref[at, :], sin_ref[at, :]
        raw_q = jnp.dot(low, w_ref[0], preferred_element_type=F32)
        raw_k = jnp.dot(low, w_ref[1], preferred_element_type=F32)
        raw_v = jnp.dot(low, w_ref[2], preferred_element_type=F32)
        out = pl.ds(pl.multiple_of(HALF + i * step, 16), step)
        for p in range(pairs):
            cols = slice(p * 128, (p + 1) * 128)
            part = raw_q[:, cols]
            qp = (part * cos + partner_lanes(part) * sin).astype(BF) * BF(HEAD_DIM**-0.5)
            qs_ref = q_all
            qs_ref[at, cols] = qp
            part = raw_k[:, cols]
            k_ref[out, cols] = (part * cos + partner_lanes(part) * sin).astype(BF)
        v_ref[out, :] = raw_v.astype(BF)
        return carry

    def run(q_scr):
        nonlocal q_all
        q_all = q_scr
        lax.fori_loop(0, ext // step, project, 0)
        q_ref[...] = q_scr[:rows, :]

    q_all = None
    pl.run_scoped(run, pltpu.VMEM((ext, width), BF))
    k_ref[:HALF, :] = k_ref[rows + HALF :, :]
    v_ref[:HALF, :] = v_ref[rows + HALF :, :]

    def block(i, carry):
        bias = window_bias(scal_ref, i, rows)
        at = pl.ds(pl.multiple_of(i * QB, QB), QB)
        keys = pl.ds(pl.multiple_of(i * QB, QB), WIN)
        for p in range(pairs):
            cols = slice(p * 128, (p + 1) * 128)
            qs = stack_heads(q_ref[at, cols])
            scores = dot(k_ref[keys, cols], qs, ((1,), (1,))) + bias
            peak = jnp.max(scores, axis=0, keepdims=True)
            raw = jnp.exp(scores - peak)
            total = jnp.sum(raw, axis=0, keepdims=True)
            probs = (raw * (1.0 / total)).astype(BF)
            both = dot(v_ref[keys, cols], probs, ((0,), (0,)))
            mixed_ref[at, cols] = unstack_columns(both).astype(BF)
            lse_ref[i, p] = peak + jnp.log(total)
        return carry

    lax.fori_loop(0, rows // QB, block, 0)


def qkv_attn(scal, norm_ext, w, cos, sin, rows):
    ext = norm_ext.shape[0]
    width = w.shape[2]
    whole = pl.BlockSpec(memory_space=pltpu.VMEM)
    return pl.pallas_call(
        qkv_attn_kernel,
        out_shape=(
            jax.ShapeDtypeStruct((rows, width), BF),
            jax.ShapeDtypeStruct((rows + 2 * HALF, width), BF),
            jax.ShapeDtypeStruct((rows + 2 * HALF, width), BF),
            jax.ShapeDtypeStruct((rows, width), BF),
            jax.ShapeDtypeStruct((rows // QB, width // 128, 1, 2 * QB), F32),
        ),
        in_specs=[pl.BlockSpec(memory_space=pltpu.SMEM)] + [whole] * 4,
        out_specs=(whole,) * 5,
        compiler_params=vmem(28),
        cost_estimate=pl.CostEstimate(
            flops=2 * ext * norm_ext.shape[1] * 3 * width + 16 * rows * WIN * width,
            bytes_accessed=8_000_000,
            transcendentals=rows * WIN * width // 64,
        ),
        name="qkv_attn",
    )(scal, norm_ext, w, cos, sin)


def attn_back_kernel(
    scal_ref, q_ref, k_ref, v_ref, dm_ref, lse_ref, cos_ref, sin_ref,
    dq_ref, dk_ref, dv_ref, dk_acc, dv_acc,
):
    rows = q_ref.shape[0]
    pairs = q_ref.shape[1] // 128
    dk_acc[...] = jnp.zeros_like(dk_acc)
    dv_acc[...] = jnp.zeros_like(dv_acc)

    def unrotate(part, at):
        return (part * cos_ref[at, :] - partner_lanes(part) * sin_ref[at, :]).astype(BF)

    def block(i, carry):
        bias = window_bias(scal_ref, i, rows)
        at = pl.ds(pl.multiple_of(i * QB, QB), QB)
        keys = pl.ds(pl.multiple_of(i * QB, QB), WIN)
        for p in range(pairs):
            cols = slice(p * 128, (p + 1) * 128)
            qs = stack_heads(q_ref[at, cols])
            ds_mixed = stack_heads(dm_ref[at, cols])
            kb = k_ref[keys, cols]
            vb = v_ref[keys, cols]
            scores = dot(kb, qs, ((1,), (1,))) + bias
            probs = jnp.exp(scores - lse_ref[i, p])
            d_probs = dot(vb, ds_mixed, ((1,), (1,)))
            row_dot = jnp.sum(probs * d_probs, axis=0, keepdims=True)
            d_scores = (probs * (d_probs - row_dot)).astype(BF)
            dk_acc[keys, cols] += dot(d_scores, qs, ((1,), (0,)))
            dv_acc[keys, cols] += dot(probs.astype(BF), ds_mixed, ((1,), (0,)))
            both = dot(kb, d_scores, ((0,), (0,)))
            dq = unstack_columns(both) * HEAD_DIM**-0.5
            dq_ref[at, cols] = unrotate(dq, at)
        return carry

    lax.fori_loop(0, rows // QB, block, 0)
    dk_acc[rows + HALF :, :] += dk_acc[:HALF, :]
    dv_acc[rows + HALF :, :] += dv_acc[:HALF, :]

    def finish(i, carry):
        at = pl.ds(pl.multiple_of(i * HALF, HALF), HALF)
        src = pl.ds(pl.multiple_of(HALF + i * HALF, HALF), HALF)
        for p in range(pairs):
            cols = slice(p * 128, (p + 1) * 128)
            dk_ref[at, cols] = unrotate(dk_acc[src, cols], at)
        dv_ref[at, :] = dv_acc[src, :].astype(BF)
        return carry

    lax.fori_loop(0, rows // HALF + 1, finish, 0)


def attn_back(scal, q, k, v, dm, lse, cos, sin):
    rows, width = q.shape
    whole = pl.BlockSpec(memory_space=pltpu.VMEM)
    return pl.pallas_call(
        attn_back_kernel,
        out_shape=(
            jax.ShapeDtypeStruct((rows, width), BF),
            jax.ShapeDtypeStruct((rows + HALF, width), BF),
            jax.ShapeDtypeStruct((rows + HALF, width), BF),
        ),
        in_specs=[pl.BlockSpec(memory_space=pltpu.SMEM)] + [whole] * 7,
        out_specs=(whole,) * 3,
        scratch_shapes=[pltpu.VMEM((rows + 2 * HALF, width), F32)] * 2,
        compiler_params=vmem(28),
        cost_estimate=pl.CostEstimate(
            flops=40 * rows * WIN * width,
            bytes_accessed=8_000_000,
            transcendentals=rows * WIN * width // 64,
        ),
        name="attn_back",
    )(scal, q, k, v, dm, lse, cos, sin)


def gelu_parts(up_in):
    cdf_part = 0.5 * (1.0 + lax.erf(up_in * 0.7071067811865476))
    gelu_out = up_in * cdf_part
    gelu_slope = cdf_part + up_in * jnp.exp(-0.5 * up_in * up_in) * 0.3989422804014327
    return (gelu_out, gelu_slope)


def mm(a, b):
    return jnp.dot(a, b, preferred_element_type=F32)


def mm_nt(a, b):
    return lax.dot_general(a, b, (((1,), (1,)), ((), ())), preferred_element_type=F32)


def mm_tn(a, b):
    return lax.dot_general(a, b, (((0,), (0,)), ((), ())), preferred_element_type=F32)


def pick(core, array, dim):
    size = array.shape[dim] // 2
    return lax.dynamic_slice_in_dim(array, core * size, size, dim)


def join(core, mine, other, dim):
    return jnp.where(
        core == 0,
        jnp.concatenate([mine, other], axis=dim),
        jnp.concatenate([other, mine], axis=dim),
    )


def fetch(core, array, dim):
    across = lax.ppermute(pick(core, array, dim), "tensor", SWAP)
    beside = lax.ppermute(across, "core", SWAP)
    return join(core, across, beside, dim)


def over_cores(core, array):
    recv = lax.ppermute(pick(1 - core, array, 0), "core", SWAP)
    return pick(core, array, 0).astype(F32) + recv.astype(F32)


def over_chips(core, array):
    chips = lax.axis_size("chip")
    rows, width = array.shape
    pieces = array.astype(BF).reshape(chips, rows // chips, width)
    pieces = lax.all_to_all(pieces, "chip", 0, 0)
    total = jnp.sum(pieces.astype(F32), axis=0).astype(BF)
    spread = jnp.broadcast_to(total[None], (chips,) + total.shape)
    full = lax.all_to_all(spread, "chip", 0, 0).reshape(rows, width)
    beside = lax.ppermute(full, "core", SWAP)
    return join(core, full, beside, 0)


def per_device(
    tokens_in, seq_lengths, norm1_gain, norm2_gain, w_qkv, w_out, w_in, w_down, out_grad
):
    rows, width = tokens_in.shape
    tensor = lax.axis_index("tensor")
    core = lax.axis_index("core")
    ff = w_in.shape[2]

    edge = jnp.where(tensor == 0, tokens_in[rows - HALF :], tokens_in[:HALF])
    halo = lax.ppermute(edge, "tensor", SWAP)
    w_qkv_x = fetch(core, w_qkv, 1)
    w_out_x = fetch(core, w_out, 0)
    w_in_x = fetch(core, w_in, 1)
    w_down_x = fetch(core, w_down, 0)

    lengths = seq_lengths[0]
    own0 = tensor * rows
    halo0 = jnp.where(tensor == 0, rows, rows - HALF)
    index = jnp.concatenate(
        [own0 + jnp.arange(rows, dtype=jnp.int32), halo0 + jnp.arange(HALF, dtype=jnp.int32)]
    )
    cos, sin = spread_tables(rows, index, lengths)
    scal = jnp.stack(
        [lengths[0], lengths[0] + lengths[1], own0, halo0]
    ).astype(jnp.int32)

    tokens_ext = jnp.concatenate([tokens_in, halo], axis=0).astype(F32)
    normed_one, factor_one = normalize(tokens_ext)
    norm1 = (normed_one * norm1_gain).astype(BF)

    q_o, k_o, v_o, mixed_o, lse_o = qkv_attn(scal, norm1, w_qkv, cos, sin, rows)
    q_x, k_x, v_x, mixed_x, lse_x = qkv_attn(scal, norm1, w_qkv_x, cos, sin, rows)

    tokens = tokens_in.astype(F32)
    residual = tokens + (mm(mixed_o, w_out) + mm(mixed_x, w_out_x))
    normed_two, factor_two = normalize(residual)
    norm2 = (normed_two * norm2_gain).astype(BF)

    def ffn(win, wdown):
        up_in = mm(norm2, win[0])
        gate = mm(norm2, win[1])
        gelu_out, gelu_slope = gelu_parts(up_in)
        act = (gelu_out * gate).astype(BF)
        share = mm(act, wdown)
        d_act = mm_nt(out_grad, wdown)
        d_up = (d_act * gate * gelu_slope).astype(BF)
        d_gate = (d_act * gelu_out).astype(BF)
        d_norm = mm_nt(d_up, win[0]) + mm_nt(d_gate, win[1])
        grads = jnp.concatenate(
            [
                mm_tn(norm2, d_up).astype(BF),
                mm_tn(norm2, d_gate).astype(BF),
                mm_tn(out_grad, act).astype(BF),
            ],
            axis=1,
        )
        return share, d_norm, grads

    share_o, d_norm2_o, ff_o = ffn(w_in, w_down)
    share_x, d_norm2_x, ff_x = ffn(w_in_x, w_down_x)
    out_tokens = (residual + (share_o + share_x)).astype(BF)

    ff_o = over_cores(core, ff_o)
    ff_x = over_cores(core, ff_x)
    ff_sum = ff_o + lax.ppermute(ff_x.astype(BF), "tensor", SWAP).astype(F32)
    ff_all = over_chips(core, ff_sum)

    d_norm2 = d_norm2_o + d_norm2_x
    grad_norm2 = jnp.sum(d_norm2 * normed_two, axis=0)
    d_res = out_grad.astype(F32) + norm_back(d_norm2, norm2_gain, normed_two, factor_two)
    d_attn = d_res.astype(BF)

    def back(q, k, v, mixed, lse, wout, wqkv):
        dm = mm_nt(d_attn, wout).astype(BF)
        dq, dk, dv = attn_back(scal, q, k, v, dm, lse, cos, sin)
        grads = jnp.concatenate(
            [
                mm_tn(norm1[:rows], dq).astype(BF),
                mm_tn(norm1, dk).astype(BF),
                mm_tn(norm1, dv).astype(BF),
                mm_tn(d_attn, mixed).astype(BF),
            ],
            axis=1,
        )
        d_norm = mm_nt(dk, wqkv[1]) + mm_nt(dv, wqkv[2])
        d_norm_q = mm_nt(dq, wqkv[0])
        return grads, d_norm, d_norm_q

    at_x, dn_x, dnq_x = back(q_x, k_x, v_x, mixed_x, lse_x, w_out_x, w_qkv_x)
    at_x = over_cores(core, at_x)
    at_recv = lax.ppermute(at_x.astype(BF), "tensor", SWAP).astype(F32)
    at_o, dn_o, dnq_o = back(q_o, k_o, v_o, mixed_o, lse_o, w_out, w_qkv)

    d_norm1_kv = dn_x + dn_o
    d_norm1_own = d_norm1_kv[:rows] + (dnq_x + dnq_o)
    d_norm1_halo = d_norm1_kv[rows:]
    grad_norm1 = jnp.sum(d_norm1_own * normed_one[:rows], axis=0) + jnp.sum(
        d_norm1_halo * normed_one[rows:], axis=0
    )
    norms = jnp.stack([grad_norm1, grad_norm2], axis=1)
    norms = norms + lax.ppermute(norms, "tensor", SWAP)
    at_o = jnp.concatenate([over_cores(core, at_o) + at_recv, over_cores(core, norms)], axis=1)
    at_all = over_chips(core, at_o)

    back_edge = lax.ppermute(d_norm1_halo, "tensor", SWAP)
    zeros = jnp.zeros((rows - HALF, width), F32)
    d_norm1 = d_norm1_own + jnp.where(
        tensor == 0,
        jnp.concatenate([zeros, back_edge], axis=0),
        jnp.concatenate([back_edge, zeros], axis=0),
    )
    in_grad = (
        d_res + norm_back(d_norm1, norm1_gain, normed_one[:rows], factor_one[:rows])
    ).astype(BF)

    heads = w_qkv.shape[2]
    grad_in = jnp.stack([ff_all[:, :ff], ff_all[:, ff : 2 * ff]]).astype(F32)
    grad_down = ff_all[:, 2 * ff :].astype(F32).T
    grad_qkv = jnp.stack([at_all[:, j * heads : (j + 1) * heads] for j in range(3)]).astype(F32)
    grad_out = at_all[:, 3 * heads : 4 * heads].astype(F32).T
    grad_norm1 = at_all[:, 4 * heads].astype(F32)
    grad_norm2 = at_all[:, 4 * heads + 1].astype(F32)
    return (out_tokens, in_grad, grad_norm1, grad_norm2, grad_qkv, grad_out, grad_in, grad_down)


def solution(mesh):
    chips = mesh.shape["dp"] // 2
    grid = Mesh(mesh.devices.reshape(chips, 2, 2), ("chip", "core", "tensor"))
    rows = P(("chip", "core", "tensor"), None)
    weights = (P(None, None, "tensor"), P("tensor", None), P(None, None, "tensor"), P("tensor", None))
    return jax.shard_map(
        per_device,
        mesh=grid,
        in_specs=(rows, P(("chip", "core"), None), P(), P(), *weights, rows),
        out_specs=(rows, rows, P(), P(), *weights),
        check_vma=False,
    )
```

```python
import functools

import jax
import jax.numpy as jnp
from jax import lax
from jax.experimental import pallas as pl
from jax.experimental.pallas import tpu as pltpu
from jax.sharding import Mesh, PartitionSpec as P

HEAD_DIM = 64
HALF = 64
QB = 128
WIN = QB + 2 * HALF
SWAP = [(0, 1), (1, 0)]
BF = jnp.bfloat16
F32 = jnp.float32


def vmem(megabytes):
    return pltpu.CompilerParams(vmem_limit_bytes=megabytes * 1024 * 1024)


def normalize(values):
    centred = values - jnp.mean(values, axis=-1, keepdims=True)
    factor = lax.rsqrt(jnp.mean(centred * centred, axis=-1, keepdims=True) + 1e-05)
    return (centred * factor, factor)


def norm_back(d_norm, gain_vec, normed, factor):
    scaled = d_norm * gain_vec
    return factor * (
        scaled
        - jnp.mean(scaled, axis=-1, keepdims=True)
        - normed * jnp.mean(scaled * normed, axis=-1, keepdims=True)
    )


def partner_lanes(values):
    lane = lax.broadcasted_iota(jnp.int32, values.shape, 1)
    lower = (lane & 32) == 0
    width = values.shape[1]
    return jnp.where(
        lower, pltpu.roll(values, width - 32, 1), pltpu.roll(values, 32, 1)
    )


def window_bias(scal_ref, block, rows):
    e0, e1, t0, h0 = scal_ref[1], scal_ref[2], scal_ref[3], scal_ref[4]
    j = block * QB + lax.broadcasted_iota(jnp.int32, (WIN, QB), 0)
    t = t0 + block * QB + lax.broadcasted_iota(jnp.int32, (WIN, QB), 1)
    u = jnp.where(
        j < HALF, h0 + j, jnp.where(j >= rows + HALF, h0 + j - rows - HALF, t0 + j - HALF)
    )
    seg_t = (t >= e0).astype(jnp.int32) + (t >= e1).astype(jnp.int32)
    seg_u = (u >= e0).astype(jnp.int32) + (u >= e1).astype(jnp.int32)
    allowed = (seg_t == seg_u) & (jnp.abs(t - u) <= HALF)
    bias = jnp.where(allowed, 0.0, -1e30).astype(F32)
    return jnp.concatenate([bias, bias], axis=1)


def stack_heads(pair):
    lower = lax.broadcasted_iota(jnp.int32, pair.shape, 1) < HEAD_DIM
    zero = jnp.zeros_like(pair)
    return jnp.concatenate(
        [jnp.where(lower, pair, zero), jnp.where(lower, zero, pair)], axis=0
    )


def unstack_columns(both):
    return jnp.concatenate(
        [both[:HEAD_DIM, :QB], both[HEAD_DIM:, QB:]], axis=0
    ).T


def dot(a, b, contract):
    return lax.dot_general(a, b, ((contract[0], contract[1]), ((), ())), preferred_element_type=F32)


class Stage:
    def __init__(self, core, sources, buffers, in_sems, results, out_bufs, out_sems):
        self.buffers, self.results, self.out_bufs, self.out_sems = (
            buffers, results, out_bufs, out_sems,
        )
        self.pending, self.sent = [], []
        sem = 0
        for refs, buffer in zip(sources, buffers):
            copies = []
            if len(refs) == 1:
                pairs = [(refs[0], buffer)]
            else:
                dim = refs[2]
                size = refs[0].shape[dim]
                pairs = []
                for ref, index in ((refs[0], core), (refs[1], 1 - core)):
                    at = [slice(None)] * len(buffer.shape)
                    at[dim] = pl.ds(pl.multiple_of(index * size, size), size)
                    pairs.append((ref, buffer.at[tuple(at)]))
            for source, target in pairs:
                copy = pltpu.make_async_copy(source, target, in_sems.at[sem])
                copy.start()
                copies.append(copy)
                sem += 1
            self.pending.append(copies)

    def take(self, *which):
        for k in which:
            for copy in self.pending[k]:
                copy.wait()
            self.pending[k] = []
        found = tuple(self.buffers[k] for k in which)
        return found if len(found) > 1 else found[0]

    def send(self, *which):
        for k in which:
            copy = pltpu.make_async_copy(self.out_bufs[k], self.results[k], self.out_sems.at[k])
            copy.start()
            self.sent.append(copy)

    def finish(self):
        for copy in self.sent:
            copy.wait()


def call(body, scalars, inputs, outs, scratch, name):
    inputs = [one if isinstance(one, tuple) else (one,) for one in inputs]
    flat, shapes = [], []
    for one in inputs:
        flat += list(one[:2])
        shape = list(one[0].shape)
        if len(one) == 3:
            shape[one[2]] *= 2
        shapes.append(pltpu.VMEM(tuple(shape), one[0].dtype))
    count, n_out, n_scal = len(flat), len(outs), len(scalars)

    def kernel(*refs):
        scal, refs = refs[:n_scal], refs[n_scal:]
        hbm, refs = refs[:count], refs[count:]
        results, refs = refs[:n_out], refs[n_out:]
        bufs, refs = refs[: len(inputs)], refs[len(inputs) :]
        out_bufs, refs = refs[:n_out], refs[n_out:]
        in_sems, out_sems, refs = refs[0], refs[1], refs[2:]
        sources, at = [], 0
        for one in inputs:
            if len(one) == 3:
                sources.append((hbm[at], hbm[at + 1], one[2]))
                at += 2
            else:
                sources.append((hbm[at],))
                at += 1
        stage = Stage(scal[0][0], sources, bufs, in_sems, results, out_bufs, out_sems)
        body(stage, scal, out_bufs, refs)
        stage.finish()

    return pl.pallas_call(
        kernel,
        out_shape=tuple(jax.ShapeDtypeStruct(shape, kind) for shape, kind in outs),
        in_specs=[pl.BlockSpec(memory_space=pltpu.SMEM)] * n_scal
        + [pl.BlockSpec(memory_space=pl.ANY)] * count,
        out_specs=(pl.BlockSpec(memory_space=pl.ANY),) * n_out,
        scratch_shapes=shapes
        + [pltpu.VMEM(shape, kind) for shape, kind in outs]
        + [pltpu.SemaphoreType.DMA((count,)), pltpu.SemaphoreType.DMA((n_out,))]
        + [pltpu.VMEM(shape, kind) for shape, kind in scratch],
        compiler_params=vmem(60),
        cost_estimate=pl.CostEstimate(flops=1000, bytes_accessed=1000, transcendentals=0),
        name=name,
    )(*scalars, *flat)


def qkv_attn(scal, w, norm=None, tables=None, tokens=None, halo=None, gain=None):
    first = tokens is not None
    width, dim = (w[0] if isinstance(w, tuple) else w).shape[2], w[0].shape[-2]
    if isinstance(w, tuple):
        dim *= 2
    rows = tokens.shape[0] if first else norm.shape[0] - HALF
    ext = rows + HALF
    pairs = width // 128
    step = 208 if ext % 208 == 0 else 64
    frequency = 10000.0 ** (-jnp.arange(0, HEAD_DIM, 2, dtype=F32) / HEAD_DIM)

    def body(stage, scalars, outs, scratch):
        (scal_ref,) = scalars
        q_ref, k_ref, v_ref, mixed_ref, mixedt_ref, lse_ref = outs[:6]
        (q_scr,) = scratch
        if first:
            norm_ref, cos_ref, sin_ref = outs[6:]
            freq_ref, tok_ref, halo_ref, gain_ref = stage.take(0, 1, 2, 3)

            def norm_rows(src_ref, src, dst):
                normed, _ = normalize(src_ref[src, :].astype(F32))
                norm_ref[dst, :] = (normed * gain_ref[...]).astype(BF)

            def norm_step(i, carry):
                at = pl.ds(pl.multiple_of(i * QB, QB), QB)
                norm_rows(tok_ref, at, at)
                return carry

            lax.fori_loop(0, rows // QB, norm_step, 0)
            norm_rows(halo_ref, slice(0, HALF), slice(rows, ext))
            stage.send(6)

            def angles(i, carry):
                at = pl.ds(pl.multiple_of(i * HALF, HALF), HALF)
                j = i * HALF + lax.broadcasted_iota(jnp.int32, (HALF, 128), 0)
                e0, e1 = scal_ref[1], scal_ref[2]
                t = jnp.where(j < rows, scal_ref[3] + j, scal_ref[4] + j - rows)
                opening = jnp.where(t >= e1, e1, jnp.where(t >= e0, e0, 0))
                angle = (t - opening).astype(F32) * freq_ref[...]
                lane = lax.broadcasted_iota(jnp.int32, (HALF, 128), 1)
                sine = jnp.sin(angle)
                cos_ref[at, :] = jnp.cos(angle)
                sin_ref[at, :] = jnp.where((lane & 32) == 0, -sine, sine)
                return carry

            lax.fori_loop(0, ext // HALF, angles, 0)
            stage.send(7, 8)
            w_ref = stage.take(4)
        else:
            norm_ref, cos_ref, sin_ref, w_ref = stage.take(0, 1, 2, 3)

        def project(i, carry):
            at = pl.ds(pl.multiple_of(i * step, 16), step)
            low = norm_ref[at, :]
            cosine, sine = cos_ref[at, :], sin_ref[at, :]
            raw_q = jnp.dot(low, w_ref[0], preferred_element_type=F32)
            raw_k = jnp.dot(low, w_ref[1], preferred_element_type=F32)
            raw_v = jnp.dot(low, w_ref[2], preferred_element_type=F32)
            out = pl.ds(pl.multiple_of(HALF + i * step, 16), step)
            for p in range(pairs):
                cols = slice(p * 128, (p + 1) * 128)
                part = raw_q[:, cols]
                turned = (part * cosine + partner_lanes(part) * sine).astype(BF)
                q_scr[at, cols] = turned * BF(HEAD_DIM**-0.5)
                part = raw_k[:, cols]
                k_ref[out, cols] = (part * cosine + partner_lanes(part) * sine).astype(BF)
            v_ref[out, :] = raw_v.astype(BF)
            return carry

        lax.fori_loop(0, ext // step, project, 0)
        q_ref[...] = q_scr[:rows, :]
        k_ref[:HALF, :] = k_ref[rows + HALF :, :]
        v_ref[:HALF, :] = v_ref[rows + HALF :, :]
        stage.send(0, 1, 2)

        def block(i, carry):
            bias = window_bias(scal_ref, i, rows)
            at = pl.ds(pl.multiple_of(i * QB, QB), QB)
            keys = pl.ds(pl.multiple_of(i * QB, QB), WIN)
            cols = [slice(p * 128, (p + 1) * 128) for p in range(pairs)]
            scores = [
                dot(k_ref[keys, c], stack_heads(q_ref[at, c]), ((1,), (1,))) + bias for c in cols
            ]
            peaks = [jnp.max(one, axis=0, keepdims=True) for one in scores]
            raws = [jnp.exp(one - peak) for one, peak in zip(scores, peaks)]
            totals = [jnp.sum(one, axis=0, keepdims=True) for one in raws]
            probs = [(one * (1.0 / total)).astype(BF) for one, total in zip(raws, totals)]
            both = [dot(v_ref[keys, c], one, ((0,), (0,))) for c, one in zip(cols, probs)]
            for p, c in enumerate(cols):
                flipped = jnp.concatenate(
                    [both[p][:HEAD_DIM, :QB], both[p][HEAD_DIM:, QB:]], axis=0
                )
                mixedt_ref[c, at] = flipped.astype(BF)
                mixed_ref[at, c] = flipped.T.astype(BF)
                lse_ref[i, p] = peaks[p] + jnp.log(totals[p])
            return carry

        lax.fori_loop(0, rows // QB, block, 0)
        stage.send(3, 4, 5)

    outs = [
        ((rows, width), BF),
        ((rows + 2 * HALF, width), BF),
        ((rows + 2 * HALF, width), BF),
        ((rows, width), BF),
        ((width, rows), BF),
        ((rows // QB, pairs, 1, 2 * QB), F32),
    ]
    if first:
        outs += [((ext, dim), BF), ((ext, 128), F32), ((ext, 128), F32)]
        inputs = [jnp.tile(frequency, 4).reshape(1, 128), tokens, halo, gain.reshape(1, dim), w]
    else:
        inputs = [norm, *tables, w]
    return call(body, [scal], inputs, outs, [((ext, width), BF)], "qkv_attn")


def store_rows(pieces, place, start, value):
    size, stop = pieces.shape[1], start + value.shape[0]
    row = start
    while row < stop:
        block, inside = divmod(row, size)
        count = min(size - inside, stop - row)
        part = value[row - start : row - start + count].astype(BF)
        pieces[block ^ place, inside : inside + count, :] = part
        row += count


def ffn(where, dy, win, wdown, gain, start=None, carry_in=None):
    last = start is None
    rows, dim = dy.shape
    ff = win[0].shape[1] * 2 if isinstance(win, tuple) else win.shape[1]
    height = -(-3 * ff // 256) * 64
    step = 256 if rows % 256 == 0 else 64

    def body(stage, scalars, outs, scratch):
        (where_ref,) = scalars
        act_s, d_s, pieces = scratch[:3]
        if last:
            n_ref, res_ref, gain_ref, win_ref, dy_ref, wd_ref, share_in, dn_in = stage.take(*range(8))
            a_ref, b_ref, out_ref, dres_ref, dattn_ref, gn_ref = outs
            gn_ref[...] = jnp.zeros_like(gn_ref)
        else:
            tok_ref, mo_ref, mx_ref, wo_ref, wx_ref, gain_ref, win_ref, dy_ref, wd_ref = stage.take(
                *range(9)
            )
            a_ref, b_ref, n_ref, res_ref, share_ref, dn_ref = outs

        def one(i, carry):
            at = pl.ds(pl.multiple_of(i * step, step), step)
            if last:
                low = n_ref[at, :]
            else:
                residual = tok_ref[at, :].astype(F32) + (
                    jnp.dot(mo_ref[at, :], wo_ref[...], preferred_element_type=F32)
                    + jnp.dot(mx_ref[at, :], wx_ref[...], preferred_element_type=F32)
                )
                res_ref[at, :] = residual
                low = (normalize(residual)[0] * gain_ref[...]).astype(BF)
                n_ref[at, :] = low
            up_in = dot(low, win_ref[0], ((1,), (1,)))
            gate = dot(low, win_ref[1], ((1,), (1,)))
            gelu_out, gelu_slope = gelu_parts(up_in)
            act = (gelu_out * gate).astype(BF)
            act_s[at, :] = act
            share = jnp.dot(act, wd_ref[...], preferred_element_type=F32)
            d_act = dot(dy_ref[at, :], wd_ref[...], ((1,), (1,)))
            d_up = (d_act * gate * gelu_slope).astype(BF)
            d_gate = (d_act * gelu_out).astype(BF)
            d_s[at, :ff] = d_up
            d_s[at, ff:] = d_gate
            dn = jnp.dot(d_up, win_ref[0], preferred_element_type=F32) + jnp.dot(
                d_gate, win_ref[1], preferred_element_type=F32
            )
            if last:
                residual = res_ref[at, :]
                out_ref[at, :] = (residual + (share_in[at, :] + share)).astype(BF)
                dn = dn + dn_in[at, :]
                normed, factor = normalize(residual)
                gn_ref[...] += jnp.sum((dn * normed).reshape(step // 8, 8, dim), axis=0)
                d_res = dy_ref[at, :].astype(F32) + norm_back(dn, gain_ref[...], normed, factor)
                dres_ref[at, :] = d_res
                dattn_ref[at, :] = d_res.astype(BF)
            else:
                share_ref[at, :] = share
                dn_ref[at, :] = dn
            return carry

        lax.fori_loop(0, rows // step, one, 0)
        stage.send(2, 3, 4, 5)
        place = where_ref[1]
        for c in range(0, 2 * ff, 384):
            value = dot(d_s[:, c : c + 384], n_ref[...], ((0,), (0,)))
            store_rows(pieces, place, c, value)
        store_rows(pieces, place, 2 * ff, dot(act_s[...], dy_ref[...], ((0,), (0,))))
        if 4 * height > 3 * ff:
            store_rows(pieces, place, 3 * ff, jnp.zeros((4 * height - 3 * ff, dim), F32))
        a_ref[...] = pieces[:2]
        b_ref[...] = pieces[2:]
        stage.send(0, 1)

    block = ((2, height, dim), BF)
    gain = gain.reshape(1, dim)
    if last:
        norm, residual, share, dn = carry_in
        inputs = [norm, residual, gain, win, dy, wdown, share, dn]
        outs = [((rows, dim), BF), ((rows, dim), F32), ((rows, dim), BF), ((8, dim), F32)]
    else:
        inputs = [*start, gain, win, dy, wdown]
        outs = [((rows, dim), BF)] + [((rows, dim), F32)] * 3
    return call(
        body,
        [where],
        inputs,
        [block, block, *outs],
        [((rows, ff), BF), ((rows, 2 * ff), BF), ((4, height, dim), BF)],
        "ffn",
    )


def attn_back(scal, where, blocks, saved, d_attn, wout, wqkv, norm, tables, earlier=None):
    q, k, v, mixed_t, lse = saved
    rows, width = q.shape
    dim = d_attn.shape[1]
    ext = rows + HALF
    pairs = width // 128
    height = dim // blocks
    step = 256 if rows % 256 == 0 else 64

    def body(stage, scalars, outs, scratch):
        where_ref, scal_ref = scalars
        a_ref, b_ref, dn_ref = outs
        dk_acc, dv_acc, dm_s, dq_s, dk_s, dv_s, pieces = scratch
        dk_acc[...] = jnp.zeros_like(dk_acc)
        dv_acc[...] = jnp.zeros_like(dv_acc)
        da_ref, wo_ref = stage.take(0, 1)

        def mix_back(i, carry):
            at = pl.ds(pl.multiple_of(i * step, step), step)
            dm_s[at, :] = dot(da_ref[at, :], wo_ref[...], ((1,), (1,))).astype(BF)
            return carry

        lax.fori_loop(0, rows // step, mix_back, 0)
        q_ref, k_ref, v_ref, lse_ref, cos_ref, sin_ref = stage.take(*range(2, 8))

        def unrotate(part, at):
            return (part * cos_ref[at, :] - partner_lanes(part) * sin_ref[at, :]).astype(BF)

        def block(i, carry):
            bias = window_bias(scal_ref, i, rows)
            at = pl.ds(pl.multiple_of(i * QB, QB), QB)
            keys = pl.ds(pl.multiple_of(i * QB, QB), WIN)
            cols = [slice(p * 128, (p + 1) * 128) for p in range(pairs)]
            qs = [stack_heads(q_ref[at, c]) for c in cols]
            dms = [stack_heads(dm_s[at, c]) for c in cols]
            scores = [dot(k_ref[keys, c], one, ((1,), (1,))) + bias for c, one in zip(cols, qs)]
            d_probs = [dot(v_ref[keys, c], one, ((1,), (1,))) for c, one in zip(cols, dms)]
            probs = [jnp.exp(one - lse_ref[i, p]) for p, one in enumerate(scores)]
            dots = [jnp.sum(a * b, axis=0, keepdims=True) for a, b in zip(probs, d_probs)]
            d_scores = [(a * (b - c)).astype(BF) for a, b, c in zip(probs, d_probs, dots)]
            d_values = [dot(a.astype(BF), b, ((1,), (0,))) for a, b in zip(probs, dms)]
            d_keys = [dot(a, b, ((1,), (0,))) for a, b in zip(d_scores, qs)]
            both = [dot(k_ref[keys, c], one, ((0,), (0,))) for c, one in zip(cols, d_scores)]
            for p, c in enumerate(cols):
                dv_acc[keys, c] += d_values[p]
                dk_acc[keys, c] += d_keys[p]
                dq_s[at, c] = unrotate(unstack_columns(both[p]) * HEAD_DIM**-0.5, at)
            return carry

        lax.fori_loop(0, rows // QB, block, 0)
        dk_acc[rows + HALF :, :] += dk_acc[:HALF, :]
        dv_acc[rows + HALF :, :] += dv_acc[:HALF, :]

        def finish(i, carry):
            at = pl.ds(pl.multiple_of(i * HALF, HALF), HALF)
            src = pl.ds(pl.multiple_of(HALF + i * HALF, HALF), HALF)
            for p in range(pairs):
                c = slice(p * 128, (p + 1) * 128)
                dk_s[at, c] = unrotate(dk_acc[src, c], at)
            dv_s[at, :] = dv_acc[src, :].astype(BF)
            return carry

        lax.fori_loop(0, ext // HALF, finish, 0)
        norm_ref, mt_ref = stage.take(8, 9)
        low = norm_ref[...]
        me = where_ref[2]
        for j, value in enumerate((dq_s, dk_s, dv_s)):
            grad = dot(low[: value.shape[0]], value[...], ((0,), (0,))).astype(BF)
            for b in range(blocks):
                pieces[b ^ me, :, j * width : (j + 1) * width] = grad[b * height : (b + 1) * height]
        grad = jnp.dot(mt_ref[...], da_ref[...], preferred_element_type=F32).astype(BF)
        for b in range(blocks):
            half, row = divmod(b, blocks // 2)
            pieces[b ^ me, :, 3 * width :] = grad[
                row * height : (row + 1) * height, half * width : (half + 1) * width
            ]
        a_ref[...] = pieces[: blocks // 2]
        b_ref[...] = pieces[blocks // 2 :]
        stage.send(0, 1)
        w_ref = stage.take(10)
        if earlier is not None:
            dn_in = stage.take(11)

        def norm_grad(at, q_too):
            dn = dot(dk_s[at, :], w_ref[1], ((1,), (1,))) + dot(dv_s[at, :], w_ref[2], ((1,), (1,)))
            if q_too:
                dn = dn + dot(dq_s[at, :], w_ref[0], ((1,), (1,)))
            if earlier is not None:
                dn = dn + dn_in[at, :]
            dn_ref[at, :] = dn

        def norm_step(i, carry):
            norm_grad(pl.ds(pl.multiple_of(i * step, step), step), True)
            return carry

        lax.fori_loop(0, rows // step, norm_step, 0)
        norm_grad(slice(rows, ext), False)
        stage.send(2)

    block = ((blocks // 2, height, 4 * width), BF)
    inputs = [d_attn, wout, q, k, v, lse, *tables, norm, mixed_t, wqkv]
    if earlier is not None:
        inputs.append(earlier)
    return call(
        body,
        [where, scal],
        inputs,
        [block, block, ((ext, dim), F32)],
        [((rows + 2 * HALF, width), F32)] * 2
        + [((rows, width), BF)] * 2
        + [((ext, width), BF)] * 2
        + [((blocks, height, 4 * width), BF)],
        "attn_back",
    )


def gelu_parts(up_in):
    cdf_part = 0.5 * (1.0 + lax.erf(up_in * 0.7071067811865476))
    gelu_out = up_in * cdf_part
    gelu_slope = cdf_part + up_in * jnp.exp(-0.5 * up_in * up_in) * 0.3989422804014327
    return (gelu_out, gelu_slope)


def together(*values):
    return lax.optimization_barrier(values)


def after(value, *others):
    return lax.optimization_barrier((value, *others))[0]


def pick(index, array, dim=0):
    size = array.shape[dim] // 2
    return lax.dynamic_slice_in_dim(array, index * size, size, dim)


def trade(array, axis):
    return lax.ppermute(array, axis, SWAP)


def add(kept, recv):
    return (kept.astype(F32) + recv.astype(F32)).astype(BF)


def add3(one, two, three):
    return (one.astype(F32) + two.astype(F32) + three.astype(F32)).astype(BF)


def adds(kept, recv):
    half = kept.shape[0] // 2
    first, second = add(kept[:half], recv[:half]), add(kept[half:], recv[half:])
    return (first[0], second[0]) if half == 1 else (first, second)


def split(results):
    return results[2], results[:2]


def flip(array, bit):
    count = lax.axis_size("hi")
    return lax.ppermute(array, "hi", [(i, i ^ bit) for i in range(count)])


def deal(array):
    count = lax.axis_size("hi")
    rows, width = array.shape
    return lax.all_to_all(array.reshape(count, rows // count, width), "hi", 0, 0)


def total(pieces):
    return jnp.sum(pieces.astype(F32), axis=0).astype(BF)


def spread_hi(piece):
    count = lax.axis_size("hi")
    full = lax.all_to_all(jnp.broadcast_to(piece[None], (count,) + piece.shape), "hi", 0, 0)
    return full.reshape((count * piece.shape[0],) + piece.shape[1:])


def assemble_ff(where, pieces, ff):
    height, dim = pieces[0].shape

    def body(stage, scalars, outs, scratch):
        (where_ref,) = scalars
        gi_ref, gd_ref = outs
        (whole,) = scratch
        for k in range(4):
            whole[where_ref[1] ^ k] = stage.take(k)[...]
        for out, index in ((0, 0), (0, 1), (1, 2)):
            row, stop = index * ff, (index + 1) * ff
            while row < stop:
                block, inside = divmod(row, height)
                count = min(height - inside, stop - row)
                part = whole[block, inside : inside + count, :].astype(F32)
                at = slice(row - index * ff, row - index * ff + count)
                if out == 0:
                    gi_ref[index, at, :] = part
                else:
                    gd_ref[at, :] = part
                row += count
        stage.send(0, 1)

    return call(
        body,
        [where],
        list(pieces),
        [((2, ff, dim), F32), ((ff, dim), F32)],
        [((4, height, dim), BF)],
        "assemble_ff",
    )


def assemble_attn(where, pieces, heads):
    count, height, width = pieces[0].shape
    blocks = 4 * count

    def body(stage, scalars, outs, scratch):
        (where_ref,) = scalars
        gq_ref, go_ref = outs
        (whole,) = scratch
        for k in range(4):
            piece = stage.take(k)
            for b in range(count):
                whole[where_ref[2] ^ (k * count + b)] = piece[b]
        for b in range(blocks):
            at = slice(b * height, (b + 1) * height)
            for j in range(3):
                gq_ref[j, at, :] = whole[b, :, j * heads : (j + 1) * heads].astype(F32)
        stage.send(0)
        for b in range(blocks):
            half, row = divmod(b, blocks // 2)
            go_ref[row * height : (row + 1) * height, half * heads : (half + 1) * heads] = whole[
                b, :, 3 * heads :
            ].astype(F32)
        stage.send(1)

    return call(
        body,
        [where],
        list(pieces),
        [((3, blocks * height, heads), F32), ((heads, 2 * heads), F32)],
        [((blocks, height, width), BF)],
        "assemble_attn",
    )


def per_device(
    tokens_in, seq_lengths, norm1_gain, norm2_gain, w_qkv, w_out, w_in, w_down, out_grad
):
    rows, width = tokens_in.shape
    tensor = lax.axis_index("tensor")
    core = lax.axis_index("core")
    lo = lax.axis_index("lo")
    place = 2 * core + lo
    chips = lax.axis_size("hi")
    hi = lax.axis_index("hi")
    w_in = jnp.swapaxes(w_in, 1, 2)
    me, bit = place, 1
    while bit < chips:
        me, bit = 2 * me + (hi // bit) % 2, 2 * bit
    where = jnp.stack([core, place, me]).astype(jnp.int32)

    edge = jnp.where(tensor == 0, tokens_in[rows - HALF :], tokens_in[:HALF])
    halo = trade(edge, "tensor")
    halo, w_qkv, w_out = together(halo, w_qkv, w_out)
    qkv_across = trade(pick(core, w_qkv, 1), "tensor")
    out_across = trade(pick(core, w_out), "tensor")

    lengths = seq_lengths[0]
    own0 = tensor * rows
    halo0 = jnp.where(tensor == 0, rows, rows - HALF)
    scal = jnp.stack([core, lengths[0], lengths[0] + lengths[1], own0, halo0]).astype(jnp.int32)

    q_o, k_o, v_o, mixed_o, mixedt_o, lse_o, norm1, *tables = qkv_attn(
        scal, w_qkv, tokens=tokens_in, halo=halo, gain=norm1_gain
    )
    qkv_across, out_across, mixed_o = together(
        after(qkv_across, mixed_o), after(out_across, mixed_o), mixed_o
    )
    in_across = trade(after(pick(core, w_in, 1), mixed_o), "tensor")
    down_across = trade(after(pick(core, w_down), mixed_o), "tensor")
    w_qkv_x = (qkv_across, trade(qkv_across, "core"), 1)
    w_out_x = (out_across, trade(out_across, "core"), 0)
    q_x, k_x, v_x, mixed_x, mixedt_x, lse_x = qkv_attn(
        scal, (w_qkv_x[0], after(w_qkv_x[1], w_out_x[1]), 1), norm=norm1, tables=tables
    )

    ffa_o, ffb_o, norm2, residual, share, dn2 = ffn(
        where, out_grad, w_in, w_down, norm2_gain,
        start=(tokens_in, mixed_o, mixed_x, w_out, w_out_x),
    )
    share, dn2, ffa_o, ffb_o, in_across, down_across = together(
        share, dn2, ffa_o, ffb_o, after(in_across, ffa_o), after(down_across, ffa_o)
    )
    ff_o = adds(ffa_o, trade(ffb_o, "core"))
    w_in_x = (in_across, trade(in_across, "core"), 1)
    w_down_x = (down_across, trade(down_across, "core"), 0)
    ffo_side = trade(ff_o[1], "lo")
    w_in_x = (w_in_x[0], after(w_in_x[1], *ff_o), 1)
    ffa_x, ffb_x, out_tokens, d_res, d_attn, gain_two = ffn(
        where, out_grad, w_in_x, w_down_x, norm2_gain, carry_in=(norm2, residual, share, dn2)
    )
    out_tokens, d_res, d_attn, gain_two, ffa_x, ffb_x, ffo_side = together(
        out_tokens, d_res, d_attn, gain_two, ffa_x, ffb_x, after(ffo_side, ffa_x)
    )
    ff_o = add(ff_o[0], ffo_side)
    ff_x = adds(ffa_x, trade(ffb_x, "core"))
    ffx_side = trade(ff_x[1], "lo")
    d_attn = after(d_attn, *ff_x, ff_o)

    dn1, (ata_x, atb_x) = split(
        attn_back(
            scal, where, 4 * chips, (q_x, k_x, v_x, mixedt_x, lse_x), d_attn, w_out_x, w_qkv_x, norm1, tables
        )
    )
    dn1, ata_x, atb_x, ffx_side = together(dn1, ata_x, atb_x, after(ffx_side, ata_x))
    ff_x = add(ff_x[0], ffx_side)
    ff_recv = trade(ff_x, "tensor")
    at_x = adds(ata_x, trade(atb_x, "core"))
    atx_side = trade(at_x[1], "lo")
    q_o = after(q_o, *at_x, ff_x)
    dn1, (ata_o, atb_o) = split(
        attn_back(
            scal, where, 4 * chips, (q_o, k_o, v_o, mixedt_o, lse_o), d_attn, w_out, w_qkv, norm1, tables, dn1
        )
    )
    dn1, ata_o, atb_o, atx_side, ff_recv = together(
        dn1, ata_o, atb_o, after(atx_side, ata_o), after(ff_recv, ata_o)
    )
    at_o = adds(ata_o, trade(atb_o, "core"))
    ato_side = trade(at_o[1], "lo")
    at_x = add(at_x[0], atx_side)
    at_recv = trade(at_x, "tensor")
    ff_all = spread_hi(total(deal(add(ff_o, ff_recv))))

    at = add3(at_o[0], ato_side, at_recv)
    bit = 1
    while bit < chips:
        half = at.shape[0] // 2
        at = add(at[:half], flip(at[half:], bit))
        bit *= 2
    while bit > 1:
        bit //= 2
        at = jnp.concatenate([at, flip(at, bit)], axis=0)

    def gather(mine):
        side = trade(mine, "lo")
        return (mine, side, trade(mine, "core"), trade(side, "core"))

    grad_in, grad_down = assemble_ff(where, gather(ff_all), w_in.shape[1])
    grad_in = jnp.swapaxes(grad_in, 1, 2)
    grad_qkv, grad_out = assemble_attn(where, gather(at), w_qkv.shape[2])

    tokens_ext = jnp.concatenate([tokens_in, halo], axis=0).astype(F32)
    normed_one, factor_one = normalize(tokens_ext)
    norms = jnp.stack([jnp.sum(dn1 * normed_one, axis=0), jnp.sum(gain_two, axis=0)])
    everywhere = ("hi", "lo", "core", "tensor")
    spread = jnp.broadcast_to(norms[None], (lax.axis_size(everywhere), 2, width))
    norms = jnp.sum(lax.all_to_all(spread, everywhere, 0, 0), axis=0)

    back_edge = trade(dn1[rows:], "tensor")
    zeros = jnp.zeros((rows - HALF, width), F32)
    d_norm1 = dn1[:rows] + jnp.where(
        tensor == 0,
        jnp.concatenate([zeros, back_edge], axis=0),
        jnp.concatenate([back_edge, zeros], axis=0),
    )
    in_grad = (
        d_res + norm_back(d_norm1, norm1_gain, normed_one[:rows], factor_one[:rows])
    ).astype(BF)
    return (out_tokens, in_grad, norms[0], norms[1], grad_qkv, grad_out, grad_in, grad_down)


def solution(mesh):
    grid = Mesh(mesh.devices.reshape(mesh.shape["dp"] // 4, 2, 2, 2), ("hi", "lo", "core", "tensor"))
    rows = P(("hi", "lo", "core", "tensor"), None)
    weights = (P(None, None, "tensor"), P("tensor", None), P(None, None, "tensor"), P("tensor", None))
    return jax.shard_map(
        per_device,
        mesh=grid,
        in_specs=(rows, P(("hi", "lo", "core"), None), P(), P(), *weights, rows),
        out_specs=(rows, rows, P(), P(), *weights),
        check_vma=False,
    )
```

```python
import jax
import jax.numpy as jnp
import numpy as np
from jax import lax
from jax.experimental import pallas as pl
from jax.experimental.pallas import tpu as pltpu
from jax.sharding import Mesh, PartitionSpec as P

HEAD_DIM = 64
HALF = 64
QB = 128
WIN = QB + 2 * HALF
SWAP = [(0, 1), (1, 0)]
BF = jnp.bfloat16
F32 = jnp.float32


def vmem(megabytes):
    return pltpu.CompilerParams(vmem_limit_bytes=megabytes * 1024 * 1024)


def normalize(values):
    centred = values - jnp.mean(values, axis=-1, keepdims=True)
    factor = lax.rsqrt(jnp.mean(centred * centred, axis=-1, keepdims=True) + 1e-05)
    return (centred * factor, factor)


def norm_back(d_norm, gain_vec, normed, factor):
    scaled = d_norm * gain_vec
    return factor * (
        scaled
        - jnp.mean(scaled, axis=-1, keepdims=True)
        - normed * jnp.mean(scaled * normed, axis=-1, keepdims=True)
    )


def partner_lanes(values):
    lane = lax.broadcasted_iota(jnp.int32, values.shape, 1)
    lower = (lane & 32) == 0
    width = values.shape[1]
    return jnp.where(
        lower, pltpu.roll(values, width - 32, 1), pltpu.roll(values, 32, 1)
    )


def window_bias(scal_ref, block, rows):
    e0, e1, t0, h0 = scal_ref[1], scal_ref[2], scal_ref[3], scal_ref[4]
    j = block * QB + lax.broadcasted_iota(jnp.int32, (WIN, QB), 0)
    t = t0 + block * QB + lax.broadcasted_iota(jnp.int32, (WIN, QB), 1)
    u = jnp.where(
        j < HALF, h0 + j, jnp.where(j >= rows + HALF, h0 + j - rows - HALF, t0 + j - HALF)
    )
    seg_t = (t >= e0).astype(jnp.int32) + (t >= e1).astype(jnp.int32)
    seg_u = (u >= e0).astype(jnp.int32) + (u >= e1).astype(jnp.int32)
    allowed = (seg_t == seg_u) & (jnp.abs(t - u) <= HALF)
    bias = jnp.where(allowed, 0.0, -1e30).astype(F32)
    return jnp.concatenate([bias, bias], axis=1)


def stack_heads(pair):
    lower = lax.broadcasted_iota(jnp.int32, pair.shape, 1) < HEAD_DIM
    zero = jnp.zeros_like(pair)
    return jnp.concatenate(
        [jnp.where(lower, pair, zero), jnp.where(lower, zero, pair)], axis=0
    )


def unstack_columns(both):
    return jnp.concatenate(
        [both[:HEAD_DIM, :QB], both[HEAD_DIM:, QB:]], axis=0
    ).T


def dot(a, b, contract):
    return lax.dot_general(a, b, ((contract[0], contract[1]), ((), ())), preferred_element_type=F32)


CHUNKS = 3


class Stage:
    def __init__(self, copies, buffers, results, out_bufs, out_sems):
        self.copies, self.buffers = copies, buffers
        self.results, self.out_bufs, self.out_sems = results, out_bufs, out_sems
        self.sent = []

    def chosen(self, which):
        for one in which:
            k, chunk = one if isinstance(one, tuple) else (one, None)
            for at, group in enumerate(self.copies[k]):
                if chunk is None or at == chunk:
                    yield from group

    def begin(self, *which):
        for copy in self.chosen(which):
            copy.start()

    def take(self, *which):
        for copy in self.chosen(which):
            copy.wait()
        found = tuple(self.buffers[one[0] if isinstance(one, tuple) else one] for one in which)
        return found if len(found) > 1 else found[0]

    def send(self, k, chunk=None, source=None):
        source = self.out_bufs[k] if source is None else source
        target = self.results[k]
        if chunk is not None:
            rows = target.shape[0] // CHUNKS
            at = pl.ds(chunk * rows, rows)
            source, target = source.at[at], target.at[at]
        copy = pltpu.make_async_copy(source, target, self.out_sems.at[k, chunk or 0])
        copy.start()
        self.sent.append(copy)

    def finish(self):
        for copy in self.sent:
            copy.wait()


def by_rows(array):
    return (array,)


def call(body, scalars, inputs, outs, scratch, name, direct=()):
    flat, shapes, total = [], [], 0
    for one in inputs:
        parts = one if isinstance(one, tuple) else (one,)
        shape = list(parts[0].shape)
        if len(parts) == 5:
            shape[0] = parts[4]
        if len(parts) >= 3:
            shape[parts[2]] *= 2
        flat += list(parts[:2])
        shapes.append(pltpu.VMEM(tuple(shape), parts[0].dtype))
    n_in, n_out, n_scal = len(flat), len(outs), len(scalars)
    buffered = [k for k in range(n_out) if k not in direct]

    def kernel(*refs):
        scal, refs = refs[:n_scal], refs[n_scal:]
        hbm, refs = refs[:n_in], refs[n_in:]
        results, refs = refs[:n_out], refs[n_out:]
        bufs, refs = refs[: len(inputs)], refs[len(inputs) :]
        held = dict(zip(buffered, refs))
        refs = refs[len(buffered) :]
        in_sems, out_sems, refs = refs[0], refs[1], refs[2:]
        copies, at, sem = [], 0, 0
        for one, buffer in zip(inputs, bufs):
            if not isinstance(one, tuple):
                pairs = [[(hbm[at], buffer)]]
                at += 1
            elif len(one) == 1:
                rows = buffer.shape[0] // CHUNKS
                cuts = [pl.ds(c * rows, rows) for c in range(CHUNKS)]
                pairs = [[(hbm[at].at[cut], buffer.at[cut])] for cut in cuts]
                at += 1
            else:
                dim, core = one[2], scal[0][0]
                size = buffer.shape[dim] // 2
                pairs = [[]]
                for ref, index in ((hbm[at], core), (hbm[at + 1], 1 - core)):
                    if len(one) == 5:
                        ref = ref.at[pl.ds(one[3], one[4])]
                    cut = [slice(None)] * len(buffer.shape)
                    cut[dim] = pl.ds(pl.multiple_of(index * size, size), size)
                    pairs[0].append((ref, buffer.at[tuple(cut)]))
                at += 2
            groups = []
            for group in pairs:
                made = []
                for source, target in group:
                    made.append(pltpu.make_async_copy(source, target, in_sems.at[sem]))
                    sem += 1
                groups.append(made)
            copies.append(groups)
        stage = Stage(copies, bufs, results, held, out_sems)
        body(stage, scal, [held.get(k) for k in range(n_out)], refs)
        stage.finish()

    return pl.pallas_call(
        kernel,
        out_shape=tuple(jax.ShapeDtypeStruct(shape, kind) for shape, kind in outs),
        in_specs=[pl.BlockSpec(memory_space=pltpu.SMEM)] * n_scal
        + [pl.BlockSpec(memory_space=pl.ANY)] * n_in,
        out_specs=(pl.BlockSpec(memory_space=pl.ANY),) * n_out,
        scratch_shapes=shapes
        + [pltpu.VMEM(*outs[k]) for k in buffered]
        + [
            pltpu.SemaphoreType.DMA((CHUNKS * len(inputs) + n_in,)),
            pltpu.SemaphoreType.DMA((n_out, CHUNKS)),
        ]
        + [pltpu.VMEM(shape, kind) for shape, kind in scratch],
        compiler_params=vmem(61),
        cost_estimate=pl.CostEstimate(flops=1000, bytes_accessed=1000, transcendentals=0),
        name=name,
    )(*scalars, *flat)


def qkv_attn(scal, w, norm=None, tables=None, tokens=None, halo=None, gain=None):
    first = tokens is not None
    width, dim = (w[0] if isinstance(w, tuple) else w).shape[2], w[0].shape[-2]
    if isinstance(w, tuple):
        dim *= 2
    rows = tokens.shape[0] if first else norm.shape[0] - HALF
    ext = rows + HALF
    pairs = width // 128
    step = 208 if ext % 208 == 0 else 64
    frequency = 10000.0 ** (-np.arange(0, HEAD_DIM, 2, dtype=np.float32) / np.float32(HEAD_DIM))

    def body(stage, scalars, outs, scratch):
        (scal_ref,) = scalars
        q_ref, k_ref, v_ref, mixedt_ref, lse_ref = outs[:5]
        (q_scr,) = scratch
        if first:
            norm_ref, cos_ref, sin_ref = outs[5:]
            stage.begin(0, 1, 2, 3, 4)
            freq_ref, tok_ref, halo_ref, gain_ref = stage.take(0, 1, 2, 3)

            def norm_rows(src_ref, src, dst):
                normed, _ = normalize(src_ref[src, :].astype(F32))
                norm_ref[dst, :] = (normed * gain_ref[...]).astype(BF)

            def norm_step(i, carry):
                at = pl.ds(pl.multiple_of(i * QB, QB), QB)
                norm_rows(tok_ref, at, at)
                return carry

            lax.fori_loop(0, rows // QB, norm_step, 0, unroll=2)
            norm_rows(halo_ref, slice(0, HALF), slice(rows, ext))
            stage.send(5)

            def angles(i, carry):
                at = pl.ds(pl.multiple_of(i * HALF, HALF), HALF)
                j = i * HALF + lax.broadcasted_iota(jnp.int32, (HALF, 128), 0)
                e0, e1 = scal_ref[1], scal_ref[2]
                t = jnp.where(j < rows, scal_ref[3] + j, scal_ref[4] + j - rows)
                opening = jnp.where(t >= e1, e1, jnp.where(t >= e0, e0, 0))
                angle = (t - opening).astype(F32) * freq_ref[...]
                lane = lax.broadcasted_iota(jnp.int32, (HALF, 128), 1)
                sine = jnp.sin(angle)
                cos_ref[at, :] = jnp.cos(angle)
                sin_ref[at, :] = jnp.where((lane & 32) == 0, -sine, sine)
                return carry

            lax.fori_loop(0, ext // HALF, angles, 0, unroll=True)
            stage.send(6)
            stage.send(7)
            w_ref = stage.take(4)
        else:
            stage.begin(0, 1, 2, 3)
            norm_ref, cos_ref, sin_ref, w_ref = stage.take(0, 1, 2, 3)

        def project(i, carry):
            at = pl.ds(pl.multiple_of(i * step, 16), step)
            low = norm_ref[at, :]
            cosine, sine = cos_ref[at, :], sin_ref[at, :]
            raw_q = jnp.dot(low, w_ref[0], preferred_element_type=F32)
            raw_k = jnp.dot(low, w_ref[1], preferred_element_type=F32)
            raw_v = jnp.dot(low, w_ref[2], preferred_element_type=F32)
            out = pl.ds(pl.multiple_of(HALF + i * step, 16), step)
            for p in range(pairs):
                cols = slice(p * 128, (p + 1) * 128)
                part = raw_q[:, cols]
                turned = (part * cosine + partner_lanes(part) * sine).astype(BF)
                q_scr[at, cols] = turned * BF(HEAD_DIM**-0.5)
                part = raw_k[:, cols]
                k_ref[out, cols] = (part * cosine + partner_lanes(part) * sine).astype(BF)
            v_ref[out, :] = raw_v.astype(BF)
            return carry

        lax.fori_loop(0, ext // step, project, 0, unroll=True)
        k_ref[:HALF, :] = k_ref[rows + HALF :, :]
        v_ref[:HALF, :] = v_ref[rows + HALF :, :]
        stage.send(0, source=q_scr.at[pl.ds(0, rows)])
        stage.send(1)
        stage.send(2)

        def block(i, carry):
            bias = window_bias(scal_ref, i, rows)
            at = pl.ds(pl.multiple_of(i * QB, QB), QB)
            keys = pl.ds(pl.multiple_of(i * QB, QB), WIN)
            cols = [slice(p * 128, (p + 1) * 128) for p in range(pairs)]
            scores = [
                dot(k_ref[keys, c], stack_heads(q_scr[at, c]), ((1,), (1,))) + bias for c in cols
            ]
            peaks = [jnp.max(one, axis=0, keepdims=True) for one in scores]
            raws = [jnp.exp(one - peak) for one, peak in zip(scores, peaks)]
            totals = [jnp.sum(one, axis=0, keepdims=True) for one in raws]
            probs = [(one * (1.0 / total)).astype(BF) for one, total in zip(raws, totals)]
            both = [dot(v_ref[keys, c], one, ((0,), (0,))) for c, one in zip(cols, probs)]
            for p, c in enumerate(cols):
                flipped = jnp.concatenate(
                    [both[p][:HEAD_DIM, :QB], both[p][HEAD_DIM:, QB:]], axis=0
                )
                mixedt_ref[c, at] = flipped.astype(BF)
                lse_ref[i, p] = peaks[p] + jnp.log(totals[p])
            return carry

        lax.fori_loop(0, rows // QB, block, 0, unroll=2)
        stage.send(3)
        stage.send(4)

    outs = [
        ((rows, width), BF),
        ((rows + 2 * HALF, width), BF),
        ((rows + 2 * HALF, width), BF),
        ((width, rows), BF),
        ((rows // QB, pairs, 1, 2 * QB), F32),
    ]
    if first:
        outs += [((ext, dim), BF), ((ext, 128), F32), ((ext, 128), F32)]
        inputs = [np.tile(frequency.astype(np.float32), 4).reshape(1, 128), tokens, halo, gain.reshape(1, dim), w]
    else:
        inputs = [norm, *tables, w]
    return call(body, [scal], inputs, outs, [((ext, width), BF)], "qkv_attn", direct=(0,))


def store_rows(pieces, place, start, value):
    size, stop = pieces.shape[1], start + value.shape[0]
    row = start
    while row < stop:
        block, inside = divmod(row, size)
        count = min(size - inside, stop - row)
        part = value[row - start : row - start + count].astype(BF)
        pieces[block ^ place, inside : inside + count, :] = part
        row += count


def ffn(where, blocks, dy, win, wdown, gain, start=None, carry_in=None):
    last = start is None
    rows, dim = dy.shape
    ff = win[0].shape[1] * 2 if isinstance(win, tuple) else win.shape[1]
    height = -(-3 * ff // 256) * 256 // blocks
    step = rows // CHUNKS

    def body(stage, scalars, outs, scratch):
        (where_ref,) = scalars
        act_s, d_s, pieces = scratch[:3]
        if last:
            win_ref, wd_ref, gain_ref, n_ref, dy_ref, res_ref, share_in, dn_in = stage.buffers
            _, _, out_ref, dres_ref, dattn_ref, gn_ref = outs
            gn_ref[...] = jnp.zeros_like(gn_ref)
            stage.begin(0, (3, 0), 1, (4, 0), 2)
            for c in range(CHUNKS):
                if c:
                    stage.begin((3, c), (4, c))
                stage.begin((5, c), (6, c), (7, c))
            stage.take(0, 1, 2)
        else:
            win_ref, wd_ref, gain_ref, wo_ref, wx_ref, mo_ref, mx_ref, tok_ref, dy_ref = stage.buffers
            _, _, n_ref, res_ref, share_ref, dn_ref = outs
            stage.begin(3, 4, 5, 6, (7, 0), 2, 0, 1, (8, 0))
            for c in range(1, CHUNKS):
                stage.begin((7, c), (8, c))
            stage.take(2, 3, 4, 5, 6)

        for c in range(CHUNKS):
            at = slice(c * step, (c + 1) * step)
            if last:
                stage.take((3, c), (4, c))
                low = n_ref[at, :]
            else:
                stage.take((7, c))
                residual = tok_ref[at, :].astype(F32) + (
                    dot(mo_ref[:, at], wo_ref[...], ((0,), (0,)))
                    + dot(mx_ref[:, at], wx_ref[...], ((0,), (0,)))
                )
                res_ref[at, :] = residual
                stage.send(3, c)
                low = (normalize(residual)[0] * gain_ref[...]).astype(BF)
                n_ref[at, :] = low
                stage.send(2, c)
                if c == 0:
                    stage.take(0, 1)
                stage.take((8, c))
            up_in = dot(low, win_ref[0], ((1,), (1,)))
            gate = dot(low, win_ref[1], ((1,), (1,)))
            gelu_out, gelu_slope = gelu_parts(up_in)
            act = (gelu_out * gate).astype(BF)
            act_s[at, :] = act
            share = jnp.dot(act, wd_ref[...], preferred_element_type=F32)
            d_act = dot(dy_ref[at, :], wd_ref[...], ((1,), (1,)))
            d_up = (d_act * gate * gelu_slope).astype(BF)
            d_gate = (d_act * gelu_out).astype(BF)
            d_s[at, :ff] = d_up
            d_s[at, ff:] = d_gate
            dn = jnp.dot(d_up, win_ref[0], preferred_element_type=F32) + jnp.dot(
                d_gate, win_ref[1], preferred_element_type=F32
            )
            if last:
                stage.take((5, c), (6, c), (7, c))
                residual = res_ref[at, :]
                out_ref[at, :] = (residual + (share_in[at, :].astype(F32) + share)).astype(BF)
                stage.send(2, c)
                dn = dn + dn_in[at, :].astype(F32)
                normed, factor = normalize(residual)
                gn_ref[...] += jnp.sum((dn * normed).reshape(step // 8, 8, dim), axis=0)
                d_res = dy_ref[at, :].astype(F32) + norm_back(dn, gain_ref[...], normed, factor)
                dres_ref[at, :] = d_res
                dattn_ref[at, :] = d_res.astype(BF)
                stage.send(3, c)
                stage.send(4, c)
            else:
                share_ref[at, :] = share.astype(BF)
                dn_ref[at, :] = dn.astype(BF)
                stage.send(4, c)
                stage.send(5, c)

        if last:
            stage.send(5)
        place = where_ref[2]
        for c in range(0, 2 * ff, 384):
            value = dot(d_s[:, c : c + 384], n_ref[...], ((0,), (0,)))
            store_rows(pieces, place, c, value)
        store_rows(pieces, place, 2 * ff, dot(act_s[...], dy_ref[...], ((0,), (0,))))
        if blocks * height > 3 * ff:
            store_rows(pieces, place, 3 * ff, jnp.zeros((blocks * height - 3 * ff, dim), F32))
        stage.send(1, source=pieces.at[pl.ds(blocks // 2, blocks // 2)])
        stage.send(0, source=pieces.at[pl.ds(0, blocks // 2)])

    block = ((blocks // 2, height, dim), BF)
    gain = gain.reshape(1, dim)
    if last:
        norm, residual, share, dn = carry_in
        inputs = [win, wdown, gain] + [by_rows(one) for one in (norm, dy, residual, share, dn)]
        outs = [((rows, dim), BF), ((rows, dim), F32), ((rows, dim), BF), ((8, dim), F32)]
    else:
        tokens, mixed_o, mixed_x, wo, wx = start
        inputs = [win, wdown, gain, wo, wx, mixed_o, mixed_x, by_rows(tokens), by_rows(dy)]
        outs = [((rows, dim), BF), ((rows, dim), F32)] + [((rows, dim), BF)] * 2
    return call(
        body,
        [where],
        inputs,
        [block, block, *outs],
        [((rows, ff), BF), ((rows, 2 * ff), BF), ((blocks, height, dim), BF)],
        "ffn",
        direct=(0, 1),
    )


def attn_back(scal, where, blocks, saved, d_attn, wout, norm, tables):
    q, k, v, mixed_t, lse = saved
    rows, width = q.shape
    dim = d_attn.shape[1]
    ext = rows + HALF
    pairs = width // 128
    height = dim // blocks
    step = rows // CHUNKS

    def body(stage, scalars, outs, scratch):
        where_ref, scal_ref = scalars
        dq_s, dk_s, dv_s = outs[2:]
        stage.begin(1, 0, *range(2, 8))
        dk_acc, dv_acc, dm_s, pieces = scratch
        dk_acc[...] = jnp.zeros_like(dk_acc)
        dv_acc[...] = jnp.zeros_like(dv_acc)
        wo_ref = stage.take(1)
        for c in range(CHUNKS):
            da_ref = stage.take((0, c))
            at = slice(c * step, (c + 1) * step)
            dm_s[at, :] = dot(da_ref[at, :], wo_ref[...], ((1,), (1,))).astype(BF)
        stage.begin(8, 9)
        q_ref, k_ref, v_ref, lse_ref, cos_ref, sin_ref = stage.take(*range(2, 8))

        def unrotate(part, at):
            return (part * cos_ref[at, :] - partner_lanes(part) * sin_ref[at, :]).astype(BF)

        def block(i, carry):
            bias = window_bias(scal_ref, i, rows)
            at = pl.ds(pl.multiple_of(i * QB, QB), QB)
            keys = pl.ds(pl.multiple_of(i * QB, QB), WIN)
            cols = [slice(p * 128, (p + 1) * 128) for p in range(pairs)]
            qs = [stack_heads(q_ref[at, c]) for c in cols]
            dms = [stack_heads(dm_s[at, c]) for c in cols]
            scores = [dot(k_ref[keys, c], one, ((1,), (1,))) + bias for c, one in zip(cols, qs)]
            d_probs = [dot(v_ref[keys, c], one, ((1,), (1,))) for c, one in zip(cols, dms)]
            probs = [jnp.exp(one - lse_ref[i, p]) for p, one in enumerate(scores)]
            dots = [jnp.sum(a * b, axis=0, keepdims=True) for a, b in zip(probs, d_probs)]
            d_scores = [(a * (b - c)).astype(BF) for a, b, c in zip(probs, d_probs, dots)]
            d_values = [dot(a.astype(BF), b, ((1,), (0,))) for a, b in zip(probs, dms)]
            d_keys = [dot(a, b, ((1,), (0,))) for a, b in zip(d_scores, qs)]
            both = [dot(k_ref[keys, c], one, ((0,), (0,))) for c, one in zip(cols, d_scores)]
            for p, c in enumerate(cols):
                dv_acc[keys, c] += d_values[p]
                dk_acc[keys, c] += d_keys[p]
                dq_s[at, c] = unrotate(unstack_columns(both[p]) * HEAD_DIM**-0.5, at)
            return carry

        lax.fori_loop(0, rows // QB, block, 0, unroll=2)
        dk_acc[rows + HALF :, :] += dk_acc[:HALF, :]
        dv_acc[rows + HALF :, :] += dv_acc[:HALF, :]

        def finish(i, carry):
            at = pl.ds(pl.multiple_of(i * HALF, HALF), HALF)
            src = pl.ds(pl.multiple_of(HALF + i * HALF, HALF), HALF)
            for p in range(pairs):
                c = slice(p * 128, (p + 1) * 128)
                dk_s[at, c] = unrotate(dk_acc[src, c], at)
            dv_s[at, :] = dv_acc[src, :].astype(BF)
            return carry

        lax.fori_loop(0, ext // HALF, finish, 0)
        for k in (2, 3, 4):
            stage.send(k)
        norm_ref, mt_ref = stage.take(8, 9)
        low = norm_ref[...]
        me = where_ref[2]
        for j, value in enumerate((dq_s, dk_s, dv_s)):
            grad = dot(low[: value.shape[0]], value[...], ((0,), (0,))).astype(BF)
            for b in range(blocks):
                pieces[b ^ me, :, j * width : (j + 1) * width] = grad[b * height : (b + 1) * height]
        grad = jnp.dot(mt_ref[...], da_ref[...], preferred_element_type=F32).astype(BF)
        for b in range(blocks):
            half, row = divmod(b, blocks // 2)
            pieces[b ^ me, :, 3 * width :] = grad[
                row * height : (row + 1) * height, half * width : (half + 1) * width
            ]
        stage.send(1, source=pieces.at[pl.ds(blocks // 2, blocks // 2)])
        stage.send(0, source=pieces.at[pl.ds(0, blocks // 2)])

    block = ((blocks // 2, height, 4 * width), BF)
    inputs = [by_rows(d_attn), wout, q, k, v, lse, *tables, norm, mixed_t]
    return call(
        body,
        [where, scal],
        inputs,
        [block, block, ((rows, width), BF), ((ext, width), BF), ((ext, width), BF)],
        [((rows + 2 * HALF, width), F32)] * 2
        + [((rows, width), BF), ((blocks, height, 4 * width), BF)],
        "attn_back",
        direct=(0, 1),
    )


def gelu_parts(up_in):
    cdf_part = 0.5 * (1.0 + lax.erf(up_in * 0.7071067811865476))
    gelu_out = up_in * cdf_part
    gelu_slope = cdf_part + up_in * jnp.exp(-0.5 * up_in * up_in) * 0.3989422804014327
    return (gelu_out, gelu_slope)


def together(*values):
    return lax.optimization_barrier(values)


def after(value, *others):
    return lax.optimization_barrier((value, *others))[0]


def pick(index, array, dim=0):
    size = array.shape[dim] // 2
    return lax.dynamic_slice_in_dim(array, index * size, size, dim)


def trade(array, axis):
    flat = array.reshape(-1, array.shape[-1])
    return lax.ppermute(flat, axis, SWAP).reshape(array.shape)


def add(kept, recv):
    return (kept.astype(F32) + recv.astype(F32)).astype(BF)


def add3(one, two, three):
    return (one.astype(F32) + two.astype(F32) + three.astype(F32)).astype(BF)


def adds(kept, recv):
    half = kept.shape[0] // 2
    return add(kept[:half], recv[:half]), add(kept[half:], recv[half:])


def halve(array, bit):
    half = array.shape[0] // 2
    return add(array[:half], flip(array[half:], bit))


def widen(array, bit):
    return jnp.concatenate([array, flip(array, bit)], axis=0)


def split(results):
    return tuple(results[2:]), results[:2]


def flip(array, bit):
    count = lax.axis_size("hi")
    flat = array.reshape(-1, array.shape[-1])
    return lax.ppermute(flat, "hi", [(i, i ^ bit) for i in range(count)]).reshape(array.shape)


def rows_back(where, grads_o, grads_x, w_o, w_x):
    rows, width = grads_o[0].shape
    dim = w_o.shape[1]
    step = rows // CHUNKS

    def body(stage, scalars, outs, scratch):
        dn_ref, halo_ref = outs
        stage.begin(*range(8))
        stage.take(*range(8))
        sides = [stage.buffers[:4], stage.buffers[4:8]]

        def back(at, which):
            total = None
            for w_ref, *grads in sides:
                for j in which:
                    one = dot(grads[j][at, :], w_ref[j], ((1,), (1,)))
                    total = one if total is None else total + one
            return total

        halo_ref[...] = back(slice(rows, rows + HALF), (1, 2))
        stage.send(1)
        for c in range(CHUNKS):
            at = slice(c * step, (c + 1) * step)
            dn_ref[at, :] = back(at, (0, 1, 2))
            stage.send(0, c)

    return call(
        body,
        [where],
        [w_o, *grads_o, w_x, *grads_x],
        [((rows, dim), F32), ((HALF, dim), F32)],
        [],
        "rows_back",
    )


def assemble_ff(where, pieces, ff):
    each, height, dim = pieces[0].shape

    def body(stage, scalars, outs, scratch):
        stage.begin(0, 1, 2, 3)
        (where_ref,) = scalars
        gi_ref, gd_ref = outs
        (whole,) = scratch
        for k in range(4):
            piece = stage.take(k)
            for b in range(each):
                whole[where_ref[2] ^ (k * each + b)] = piece[b]
        for out, index in ((0, 0), (0, 1), (1, 2)):
            row, stop = index * ff, (index + 1) * ff
            while row < stop:
                block, inside = divmod(row, height)
                count = min(height - inside, stop - row)
                part = whole[block, inside : inside + count, :].astype(F32)
                at = slice(row - index * ff, row - index * ff + count)
                if out == 0:
                    gi_ref[index, at, :] = part
                else:
                    gd_ref[at, :] = part
                row += count
        stage.send(0)
        stage.send(1)

    return call(
        body,
        [where],
        list(pieces),
        [((2, ff, dim), F32), ((ff, dim), F32)],
        [((4 * each, height, dim), BF)],
        "assemble_ff",
    )


def assemble_attn(where, pieces, heads):
    count, height, width = pieces[0].shape
    blocks = 4 * count

    def body(stage, scalars, outs, scratch):
        stage.begin(0, 1, 2, 3)
        (where_ref,) = scalars
        gq_ref, go_ref = outs
        (whole,) = scratch
        for k in range(4):
            piece = stage.take(k)
            for b in range(count):
                whole[where_ref[2] ^ (k * count + b)] = piece[b]
        for b in range(blocks):
            at = slice(b * height, (b + 1) * height)
            for j in range(3):
                gq_ref[j, at, :] = whole[b, :, j * heads : (j + 1) * heads].astype(F32)
        stage.send(0)
        for b in range(blocks):
            half, row = divmod(b, blocks // 2)
            go_ref[row * height : (row + 1) * height, half * heads : (half + 1) * heads] = whole[
                b, :, 3 * heads :
            ].astype(F32)
        stage.send(1)

    return call(
        body,
        [where],
        list(pieces),
        [((3, blocks * height, heads), F32), ((heads, 2 * heads), F32)],
        [((blocks, height, width), BF)],
        "assemble_attn",
    )


def per_device(
    tokens_in, seq_lengths, norm1_gain, norm2_gain, w_qkv, w_out, w_in, w_down, out_grad
):
    rows, width = tokens_in.shape
    tensor = lax.axis_index("tensor")
    core = lax.axis_index("core")
    lo = lax.axis_index("lo")
    place = 2 * core + lo
    chips = lax.axis_size("hi")
    hi = lax.axis_index("hi")
    w_in = jnp.swapaxes(w_in, 1, 2)
    me, bit = place, 1
    while bit < chips:
        me, bit = 2 * me + (hi // bit) % 2, 2 * bit
    where = jnp.stack([core, place, me]).astype(jnp.int32)

    edge = jnp.where(tensor == 0, tokens_in[rows - HALF :], tokens_in[:HALF])
    halo = trade(edge, "tensor")
    picked = pick(core, w_qkv, 1)
    halo, picked, where = together(halo, picked, where)
    qkv_across = trade(picked, "tensor")

    lengths = seq_lengths[0]
    own0 = tensor * rows
    halo0 = jnp.where(tensor == 0, rows, rows - HALF)
    scal = jnp.stack([core, lengths[0], lengths[0] + lengths[1], own0, halo0]).astype(jnp.int32)

    q_o, k_o, v_o, mixed_o, lse_o, norm1, *tables = qkv_attn(
        scal, w_qkv, tokens=tokens_in, halo=halo, gain=norm1_gain
    )
    qkv_across, mixed_o = together(after(qkv_across, mixed_o), mixed_o)
    w_qkv_x = (qkv_across, trade(qkv_across, "core"), 1)
    rows_across = jnp.concatenate([pick(core, w_out), pick(core, w_down)], axis=0)
    rows_across = trade(after(rows_across, mixed_o), "tensor")
    q_x, k_x, v_x, mixed_x, lse_x = qkv_attn(
        scal, w_qkv_x, norm=norm1, tables=tables
    )
    in_across = trade(after(pick(core, w_in, 1), mixed_x), "tensor")
    rows_across = after(rows_across, mixed_x)
    rows_beside = trade(rows_across, "core")
    split_at, split_rest = w_out.shape[0] // 2, w_down.shape[0] // 2
    w_out_x = (rows_across, rows_beside, 0, 0, split_at)
    w_down_x = (rows_across, rows_beside, 0, split_at, split_rest)

    ffa_o, ffb_o, norm2, residual, share, dn2 = ffn(
        where, 4 * chips, out_grad, w_in, w_down, norm2_gain,
        start=(tokens_in, mixed_o, mixed_x, w_out, w_out_x),
    )
    share, dn2, ffa_o, ffb_o, in_across = together(
        share, dn2, ffa_o, ffb_o, after(in_across, ffa_o)
    )
    ff_o = adds(ffa_o, trade(ffb_o, "core"))
    w_in_x = (in_across, trade(in_across, "core"), 1)
    ffo_side = trade(ff_o[1], "lo")
    w_in_x = (w_in_x[0], after(w_in_x[1], *ff_o), 1)
    ffa_x, ffb_x, out_tokens, d_res, d_attn, gain_two = ffn(
        where, 4 * chips, out_grad, w_in_x, w_down_x, norm2_gain, carry_in=(norm2, residual, share, dn2)
    )
    out_tokens, d_res, d_attn, gain_two, ffa_x, ffb_x, ffo_side = together(
        out_tokens, d_res, d_attn, gain_two, ffa_x, ffb_x, after(ffo_side, ffa_x)
    )
    ff_o = adds(ff_o[0], ffo_side)
    ffo_side = flip(ff_o[1], 1)
    ff_x = adds(ffa_x, trade(ffb_x, "core"))
    ffx_side = trade(ff_x[1], "lo")
    d_attn = after(d_attn, *ff_x, *ff_o)

    grads_x, (ata_x, atb_x) = split(
        attn_back(
            scal, where, 4 * chips, (q_x, k_x, v_x, mixed_x, lse_x), d_attn, w_out_x, norm1, tables
        )
    )
    ata_x, atb_x, ffx_side, ffo_side = together(
        ata_x, atb_x, after(ffx_side, ata_x), after(ffo_side, ata_x)
    )
    ff_x = adds(ff_x[0], ffx_side)
    ffx_side = flip(ff_x[1], 1)
    ff_o = add(ff_o[0], ffo_side)
    at_x = adds(ata_x, trade(atb_x, "core"))
    atx_side = trade(at_x[1], "lo")
    q_o = after(q_o, *at_x, *ff_x)
    grads_o, (ata_o, atb_o) = split(
        attn_back(
            scal, where, 4 * chips, (q_o, k_o, v_o, mixed_o, lse_o), d_attn, w_out, norm1, tables
        )
    )
    ata_o, atb_o, atx_side, ffx_side = together(
        ata_o, atb_o, after(atx_side, ata_o), after(ffx_side, ata_o)
    )
    ff_recv = trade(add(ff_x[0], ffx_side), "tensor")
    at_x = add(at_x[0], atx_side)
    at_recv = trade(at_x, "tensor")
    at_o = adds(ata_o, trade(atb_o, "core"))
    ato_side = trade(at_o[1], "lo")
    at = add3(at_o[0], ato_side, at_recv)
    dn1, dn1_halo = rows_back(
        where, grads_o, (after(grads_x[0], at), *grads_x[1:]), w_qkv, w_qkv_x
    )
    ff_all, bit = add(ff_o, after(ff_recv, at)), 2
    while bit < chips:
        ff_all, bit = halve(ff_all, bit), 2 * bit
    while bit > 1:
        bit //= 2
        ff_all = widen(ff_all, bit)

    half = at.shape[0] // 2
    at = add(at[:half], after(flip(at[half:], 1), dn1))
    dn1, dn1_halo = after(dn1, at), after(dn1_halo, at)

    tokens_ext = jnp.concatenate([after(tokens_in, dn1), halo], axis=0).astype(F32)
    normed_one, factor_one = normalize(tokens_ext)
    gain_one = jnp.sum(dn1 * normed_one[:rows], axis=0) + jnp.sum(dn1_halo * normed_one[rows:], axis=0)
    norms = jnp.stack([gain_one, jnp.sum(gain_two, axis=0)])
    back_edge = trade(dn1_halo, "tensor")
    zeros = jnp.zeros((rows - HALF, width), F32)
    d_norm1 = dn1 + jnp.where(
        tensor == 0,
        jnp.concatenate([zeros, back_edge], axis=0),
        jnp.concatenate([back_edge, zeros], axis=0),
    )
    in_grad = (
        d_res + norm_back(d_norm1, norm1_gain, normed_one[:rows], factor_one[:rows])
    ).astype(BF)
    bit = 2
    while bit < chips:
        half = at.shape[0] // 2
        at = add(at[:half], after(flip(at[half:], bit), norms))
        bit *= 2
    everywhere = ("hi", "lo", "core", "tensor")
    spread = jnp.broadcast_to(norms[None], (lax.axis_size(everywhere), 2, width))
    norms = jnp.sum(lax.all_to_all(spread, everywhere, 0, 0), axis=0)

    while bit > 1:
        bit //= 2
        at = widen(at, bit)

    def gather(mine, *others):
        side = after(trade(mine, "lo"), *others)
        return (mine, side, trade(mine, "core"), trade(side, "core"))

    grad_in, grad_down = assemble_ff(where, gather(ff_all), w_in.shape[1])
    grad_in = jnp.swapaxes(grad_in, 1, 2)
    grad_qkv, grad_out = assemble_attn(where, gather(at, grad_down, in_grad, norms), w_qkv.shape[2])

    return (out_tokens, in_grad, norms[0], norms[1], grad_qkv, grad_out, grad_in, grad_down)


def solution(mesh):
    grid = Mesh(mesh.devices.reshape(mesh.shape["dp"] // 4, 2, 2, 2), ("hi", "lo", "core", "tensor"))
    rows = P(("hi", "lo", "core", "tensor"), None)
    weights = (P(None, None, "tensor"), P("tensor", None), P(None, None, "tensor"), P("tensor", None))
    return jax.shard_map(
        per_device,
        mesh=grid,
        in_specs=(rows, P(("hi", "lo", "core"), None), P(), P(), *weights, rows),
        out_specs=(rows, rows, P(), P(), *weights),
        check_vma=False,
    )
```

```python
import jax
import jax.numpy as jnp
import numpy as np
from jax import lax
from jax.experimental import pallas as pl
from jax.experimental.pallas import tpu as pltpu
from jax.sharding import Mesh, PartitionSpec as P

HEAD_DIM = 64
HALF = 64
QB = 128
WIN = QB + 2 * HALF
SWAP = [(0, 1), (1, 0)]
BF = jnp.bfloat16
F32 = jnp.float32


def vmem(megabytes):
    return pltpu.CompilerParams(vmem_limit_bytes=megabytes * 1024 * 1024)


def normalize(values):
    centred = values - jnp.mean(values, axis=-1, keepdims=True)
    factor = lax.rsqrt(jnp.mean(centred * centred, axis=-1, keepdims=True) + 1e-05)
    return (centred * factor, factor)


def norm_back(d_norm, gain_vec, normed, factor):
    scaled = d_norm * gain_vec
    return factor * (
        scaled
        - jnp.mean(scaled, axis=-1, keepdims=True)
        - normed * jnp.mean(scaled * normed, axis=-1, keepdims=True)
    )


def partner_lanes(values):
    lane = lax.broadcasted_iota(jnp.int32, values.shape, 1)
    lower = (lane & 32) == 0
    width = values.shape[1]
    return jnp.where(
        lower, pltpu.roll(values, width - 32, 1), pltpu.roll(values, 32, 1)
    )


def window_bias(scal_ref, block, rows):
    e0, e1, t0, h0 = scal_ref[1], scal_ref[2], scal_ref[3], scal_ref[4]
    j = block * QB + lax.broadcasted_iota(jnp.int32, (WIN, QB), 0)
    t = t0 + block * QB + lax.broadcasted_iota(jnp.int32, (WIN, QB), 1)
    u = jnp.where(
        j < HALF, h0 + j, jnp.where(j >= rows + HALF, h0 + j - rows - HALF, t0 + j - HALF)
    )
    seg_t = (t >= e0).astype(jnp.int32) + (t >= e1).astype(jnp.int32)
    seg_u = (u >= e0).astype(jnp.int32) + (u >= e1).astype(jnp.int32)
    allowed = (seg_t == seg_u) & (jnp.abs(t - u) <= HALF)
    bias = jnp.where(allowed, 0.0, -1e30).astype(F32)
    return jnp.concatenate([bias, bias], axis=1)


def stack_heads(pair):
    lower = lax.broadcasted_iota(jnp.int32, pair.shape, 1) < HEAD_DIM
    zero = jnp.zeros_like(pair)
    return jnp.concatenate(
        [jnp.where(lower, pair, zero), jnp.where(lower, zero, pair)], axis=0
    )


def unstack_columns(both):
    return jnp.concatenate(
        [both[:HEAD_DIM, :QB], both[HEAD_DIM:, QB:]], axis=0
    ).T


def dot(a, b, contract):
    return lax.dot_general(a, b, ((contract[0], contract[1]), ((), ())), preferred_element_type=F32)


CHUNKS = 3


class Stage:
    def __init__(self, copies, buffers, results, out_bufs, out_sems):
        self.copies, self.buffers = copies, buffers
        self.results, self.out_bufs, self.out_sems = results, out_bufs, out_sems
        self.sent = []

    def chosen(self, which):
        for one in which:
            k, chunk = one if isinstance(one, tuple) else (one, None)
            for at, group in enumerate(self.copies[k]):
                if chunk is None or at == chunk:
                    yield from group

    def begin(self, *which):
        for copy in self.chosen(which):
            copy.start()

    def take(self, *which):
        for copy in self.chosen(which):
            copy.wait()
        found = tuple(self.buffers[one[0] if isinstance(one, tuple) else one] for one in which)
        return found if len(found) > 1 else found[0]

    def send(self, k, chunk=None, source=None):
        source = self.out_bufs[k] if source is None else source
        target = self.results[k]
        if chunk is not None:
            rows = target.shape[0] // CHUNKS
            at = pl.ds(chunk * rows, rows)
            source, target = source.at[at], target.at[at]
        copy = pltpu.make_async_copy(source, target, self.out_sems.at[k, chunk or 0])
        copy.start()
        self.sent.append(copy)

    def finish(self):
        for copy in self.sent:
            copy.wait()


def by_rows(array):
    return (array,)


def call(body, scalars, inputs, outs, scratch, name, direct=()):
    flat, shapes, total = [], [], 0
    for one in inputs:
        parts = one if isinstance(one, tuple) else (one,)
        shape = list(parts[0].shape)
        if len(parts) == 5:
            shape[0] = parts[4]
        if len(parts) >= 3:
            shape[parts[2]] *= 2
        flat += list(parts[:2])
        shapes.append(pltpu.VMEM(tuple(shape), parts[0].dtype))
    n_in, n_out, n_scal = len(flat), len(outs), len(scalars)
    buffered = [k for k in range(n_out) if k not in direct]

    def kernel(*refs):
        scal, refs = refs[:n_scal], refs[n_scal:]
        hbm, refs = refs[:n_in], refs[n_in:]
        results, refs = refs[:n_out], refs[n_out:]
        bufs, refs = refs[: len(inputs)], refs[len(inputs) :]
        held = dict(zip(buffered, refs))
        refs = refs[len(buffered) :]
        in_sems, out_sems, refs = refs[0], refs[1], refs[2:]
        copies, at, sem = [], 0, 0
        for one, buffer in zip(inputs, bufs):
            if not isinstance(one, tuple):
                pairs = [[(hbm[at], buffer)]]
                at += 1
            elif len(one) == 1:
                rows = buffer.shape[0] // CHUNKS
                cuts = [pl.ds(c * rows, rows) for c in range(CHUNKS)]
                pairs = [[(hbm[at].at[cut], buffer.at[cut])] for cut in cuts]
                at += 1
            else:
                dim, core = one[2], scal[0][0]
                size = buffer.shape[dim] // 2
                pairs = [[]]
                for ref, index in ((hbm[at], core), (hbm[at + 1], 1 - core)):
                    if len(one) == 5:
                        ref = ref.at[pl.ds(one[3], one[4])]
                    cut = [slice(None)] * len(buffer.shape)
                    cut[dim] = pl.ds(pl.multiple_of(index * size, size), size)
                    pairs[0].append((ref, buffer.at[tuple(cut)]))
                at += 2
            groups = []
            for group in pairs:
                made = []
                for source, target in group:
                    made.append(pltpu.make_async_copy(source, target, in_sems.at[sem]))
                    sem += 1
                groups.append(made)
            copies.append(groups)
        stage = Stage(copies, bufs, results, held, out_sems)
        body(stage, scal, [held.get(k) for k in range(n_out)], refs)
        stage.finish()

    return pl.pallas_call(
        kernel,
        out_shape=tuple(jax.ShapeDtypeStruct(shape, kind) for shape, kind in outs),
        in_specs=[pl.BlockSpec(memory_space=pltpu.SMEM)] * n_scal
        + [pl.BlockSpec(memory_space=pl.ANY)] * n_in,
        out_specs=(pl.BlockSpec(memory_space=pl.ANY),) * n_out,
        scratch_shapes=shapes
        + [pltpu.VMEM(*outs[k]) for k in buffered]
        + [
            pltpu.SemaphoreType.DMA((CHUNKS * len(inputs) + n_in,)),
            pltpu.SemaphoreType.DMA((n_out, CHUNKS)),
        ]
        + [pltpu.VMEM(shape, kind) for shape, kind in scratch],
        compiler_params=vmem(61),
        cost_estimate=pl.CostEstimate(flops=1000, bytes_accessed=1000, transcendentals=0),
        name=name,
    )(*scalars, *flat)


def qkv_attn(scal, w, norm=None, tables=None, tokens=None, halo=None, gain=None):
    first = tokens is not None
    width, dim = (w[0] if isinstance(w, tuple) else w).shape[2], w[0].shape[-2]
    if isinstance(w, tuple):
        dim *= 2
    rows = tokens.shape[0] if first else norm.shape[0] - HALF
    ext = rows + HALF
    pairs = width // 128
    step = 208 if ext % 208 == 0 else 64
    frequency = 10000.0 ** (-np.arange(0, HEAD_DIM, 2, dtype=np.float32) / np.float32(HEAD_DIM))

    def body(stage, scalars, outs, scratch):
        (scal_ref,) = scalars
        q_ref, k_ref, v_ref, mixedt_ref, lse_ref = outs[:5]
        (q_scr,) = scratch
        if first:
            norm_ref, cos_ref, sin_ref = outs[5:]
            stage.begin(0, 1, 2, 3, 4)
            freq_ref, tok_ref, halo_ref, gain_ref = stage.take(0, 1, 2, 3)

            def norm_rows(src_ref, src, dst):
                normed, _ = normalize(src_ref[src, :].astype(F32))
                norm_ref[dst, :] = (normed * gain_ref[...]).astype(BF)

            def norm_step(i, carry):
                at = pl.ds(pl.multiple_of(i * QB, QB), QB)
                norm_rows(tok_ref, at, at)
                return carry

            lax.fori_loop(0, rows // QB, norm_step, 0, unroll=2)
            norm_rows(halo_ref, slice(0, HALF), slice(rows, ext))
            stage.send(5)

            def angles(i, carry):
                at = pl.ds(pl.multiple_of(i * HALF, HALF), HALF)
                j = i * HALF + lax.broadcasted_iota(jnp.int32, (HALF, 128), 0)
                e0, e1 = scal_ref[1], scal_ref[2]
                t = jnp.where(j < rows, scal_ref[3] + j, scal_ref[4] + j - rows)
                opening = jnp.where(t >= e1, e1, jnp.where(t >= e0, e0, 0))
                angle = (t - opening).astype(F32) * freq_ref[...]
                lane = lax.broadcasted_iota(jnp.int32, (HALF, 128), 1)
                sine = jnp.sin(angle)
                cos_ref[at, :] = jnp.cos(angle)
                sin_ref[at, :] = jnp.where((lane & 32) == 0, -sine, sine)
                return carry

            lax.fori_loop(0, ext // HALF, angles, 0, unroll=True)
            stage.send(6)
            stage.send(7)
            w_ref = stage.take(4)
        else:
            stage.begin(0, 1, 2, 3)
            norm_ref, cos_ref, sin_ref, w_ref = stage.take(0, 1, 2, 3)

        def project(i, carry):
            at = pl.ds(pl.multiple_of(i * step, 16), step)
            low = norm_ref[at, :]
            cosine, sine = cos_ref[at, :], sin_ref[at, :]
            raw_q = jnp.dot(low, w_ref[0], preferred_element_type=F32)
            raw_k = jnp.dot(low, w_ref[1], preferred_element_type=F32)
            raw_v = jnp.dot(low, w_ref[2], preferred_element_type=F32)
            out = pl.ds(pl.multiple_of(HALF + i * step, 16), step)
            for p in range(pairs):
                cols = slice(p * 128, (p + 1) * 128)
                part = raw_q[:, cols]
                turned = (part * cosine + partner_lanes(part) * sine).astype(BF)
                q_scr[at, cols] = turned * BF(HEAD_DIM**-0.5)
                part = raw_k[:, cols]
                k_ref[out, cols] = (part * cosine + partner_lanes(part) * sine).astype(BF)
            v_ref[out, :] = raw_v.astype(BF)
            return carry

        lax.fori_loop(0, ext // step, project, 0, unroll=True)
        k_ref[:HALF, :] = k_ref[rows + HALF :, :]
        v_ref[:HALF, :] = v_ref[rows + HALF :, :]
        stage.send(0, source=q_scr.at[pl.ds(0, rows)])
        stage.send(1)
        stage.send(2)

        def block(i, carry):
            bias = window_bias(scal_ref, i, rows)
            at = pl.ds(pl.multiple_of(i * QB, QB), QB)
            keys = pl.ds(pl.multiple_of(i * QB, QB), WIN)
            cols = [slice(p * 128, (p + 1) * 128) for p in range(pairs)]
            scores = [
                dot(k_ref[keys, c], stack_heads(q_scr[at, c]), ((1,), (1,))) + bias for c in cols
            ]
            peaks = [jnp.max(one, axis=0, keepdims=True) for one in scores]
            raws = [jnp.exp(one - peak) for one, peak in zip(scores, peaks)]
            totals = [jnp.sum(one, axis=0, keepdims=True) for one in raws]
            probs = [(one * (1.0 / total)).astype(BF) for one, total in zip(raws, totals)]
            both = [dot(v_ref[keys, c], one, ((0,), (0,))) for c, one in zip(cols, probs)]
            for p, c in enumerate(cols):
                flipped = jnp.concatenate(
                    [both[p][:HEAD_DIM, :QB], both[p][HEAD_DIM:, QB:]], axis=0
                )
                mixedt_ref[c, at] = flipped.astype(BF)
                lse_ref[i, p] = peaks[p] + jnp.log(totals[p])
            return carry

        lax.fori_loop(0, rows // QB, block, 0, unroll=2)
        stage.send(3)
        stage.send(4)

    outs = [
        ((rows, width), BF),
        ((rows + 2 * HALF, width), BF),
        ((rows + 2 * HALF, width), BF),
        ((width, rows), BF),
        ((rows // QB, pairs, 1, 2 * QB), F32),
    ]
    if first:
        outs += [((ext, dim), BF), ((ext, 128), F32), ((ext, 128), F32)]
        inputs = [np.tile(frequency.astype(np.float32), 4).reshape(1, 128), tokens, halo, gain.reshape(1, dim), w]
    else:
        inputs = [norm, *tables, w]
    return call(body, [scal], inputs, outs, [((ext, width), BF)], "qkv_attn", direct=(0,))


def store_rows(pieces, place, start, value):
    size, stop = pieces.shape[1], start + value.shape[0]
    row = start
    while row < stop:
        block, inside = divmod(row, size)
        count = min(size - inside, stop - row)
        part = value[row - start : row - start + count].astype(BF)
        pieces[block ^ place, inside : inside + count, :] = part
        row += count


def ffn(where, blocks, dy, win, wdown, gain, start=None, carry_in=None):
    last = start is None
    rows, dim = dy.shape
    ff = win[0].shape[1] * 2 if isinstance(win, tuple) else win.shape[1]
    height = -(-3 * ff // 256) * 256 // blocks
    step = rows // CHUNKS

    def body(stage, scalars, outs, scratch):
        (where_ref,) = scalars
        act_s, d_s, pieces = scratch[:3]
        if last:
            win_ref, wd_ref, gain_ref, n_ref, dy_ref, res_ref, share_in, dn_in = stage.buffers
            _, _, out_ref, dres_ref, dattn_ref, gn_ref = outs
            gn_ref[...] = jnp.zeros_like(gn_ref)
            stage.begin(0, (3, 0), 1, (4, 0), 2)
            for c in range(CHUNKS):
                if c:
                    stage.begin((3, c), (4, c))
                stage.begin((5, c), (6, c), (7, c))
            stage.take(0, 1, 2)
        else:
            win_ref, wd_ref, gain_ref, wo_ref, wx_ref, mo_ref, mx_ref, tok_ref, dy_ref = stage.buffers
            _, _, n_ref, res_ref, share_ref, dn_ref = outs
            stage.begin(3, 4, 5, 6, (7, 0), 2, 0, 1, (8, 0))
            for c in range(1, CHUNKS):
                stage.begin((7, c), (8, c))
            stage.take(2, 3, 4, 5, 6)

        for c in range(CHUNKS):
            at = slice(c * step, (c + 1) * step)
            if last:
                stage.take((3, c), (4, c))
                low = n_ref[at, :]
            else:
                stage.take((7, c))
                residual = tok_ref[at, :].astype(F32) + (
                    dot(mo_ref[:, at], wo_ref[...], ((0,), (0,)))
                    + dot(mx_ref[:, at], wx_ref[...], ((0,), (0,)))
                )
                res_ref[at, :] = residual
                stage.send(3, c)
                low = (normalize(residual)[0] * gain_ref[...]).astype(BF)
                n_ref[at, :] = low
                stage.send(2, c)
                if c == 0:
                    stage.take(0, 1)
                stage.take((8, c))
            up_in = dot(low, win_ref[0], ((1,), (1,)))
            gate = dot(low, win_ref[1], ((1,), (1,)))
            gelu_out, gelu_slope = gelu_parts(up_in)
            act = (gelu_out * gate).astype(BF)
            act_s[at, :] = act
            share = jnp.dot(act, wd_ref[...], preferred_element_type=F32)
            d_act = dot(dy_ref[at, :], wd_ref[...], ((1,), (1,)))
            d_up = (d_act * gate * gelu_slope).astype(BF)
            d_gate = (d_act * gelu_out).astype(BF)
            d_s[at, :ff] = d_up
            d_s[at, ff:] = d_gate
            dn = jnp.dot(d_up, win_ref[0], preferred_element_type=F32) + jnp.dot(
                d_gate, win_ref[1], preferred_element_type=F32
            )
            if last:
                stage.take((5, c), (6, c), (7, c))
                residual = res_ref[at, :]
                out_ref[at, :] = (residual + (share_in[at, :].astype(F32) + share)).astype(BF)
                stage.send(2, c)
                dn = dn + dn_in[at, :].astype(F32)
                normed, factor = normalize(residual)
                gn_ref[...] += jnp.sum((dn * normed).reshape(step // 8, 8, dim), axis=0)
                d_res = dy_ref[at, :].astype(F32) + norm_back(dn, gain_ref[...], normed, factor)
                dres_ref[at, :] = d_res
                dattn_ref[at, :] = d_res.astype(BF)
                stage.send(3, c)
                stage.send(4, c)
            else:
                share_ref[at, :] = share.astype(BF)
                dn_ref[at, :] = dn.astype(BF)
                stage.send(4, c)
                stage.send(5, c)

        if last:
            stage.send(5)
        place = where_ref[2]
        for c in range(0, 2 * ff, 384):
            value = dot(d_s[:, c : c + 384], n_ref[...], ((0,), (0,)))
            store_rows(pieces, place, c, value)
        store_rows(pieces, place, 2 * ff, dot(act_s[...], dy_ref[...], ((0,), (0,))))
        if blocks * height > 3 * ff:
            store_rows(pieces, place, 3 * ff, jnp.zeros((blocks * height - 3 * ff, dim), F32))
        stage.send(1, source=pieces.at[pl.ds(blocks // 2, blocks // 2)])
        stage.send(0, source=pieces.at[pl.ds(0, blocks // 2)])

    block = ((blocks // 2, height, dim), BF)
    gain = gain.reshape(1, dim)
    if last:
        norm, residual, share, dn = carry_in
        inputs = [win, wdown, gain] + [by_rows(one) for one in (norm, dy, residual, share, dn)]
        outs = [((rows, dim), BF), ((rows, dim), F32), ((rows, dim), BF), ((8, dim), F32)]
    else:
        tokens, mixed_o, mixed_x, wo, wx = start
        inputs = [win, wdown, gain, wo, wx, mixed_o, mixed_x, by_rows(tokens), by_rows(dy)]
        outs = [((rows, dim), BF), ((rows, dim), F32)] + [((rows, dim), BF)] * 2
    return call(
        body,
        [where],
        inputs,
        [block, block, *outs],
        [((rows, ff), BF), ((rows, 2 * ff), BF), ((blocks, height, dim), BF)],
        "ffn",
        direct=(0, 1),
    )


def attn_back(scal, where, blocks, saved, d_attn, wout, norm, tables):
    q, k, v, mixed_t, lse = saved
    rows, width = q.shape
    dim = d_attn.shape[1]
    ext = rows + HALF
    pairs = width // 128
    height = dim // blocks
    step = rows // CHUNKS

    def body(stage, scalars, outs, scratch):
        where_ref, scal_ref = scalars
        dq_s, dk_s, dv_s = outs[2:]
        stage.begin(1, 0, *range(2, 8))
        dk_acc, dv_acc, dm_s, pieces = scratch
        dk_acc[...] = jnp.zeros_like(dk_acc)
        dv_acc[...] = jnp.zeros_like(dv_acc)
        wo_ref = stage.take(1)
        for c in range(CHUNKS):
            da_ref = stage.take((0, c))
            at = slice(c * step, (c + 1) * step)
            dm_s[at, :] = dot(da_ref[at, :], wo_ref[...], ((1,), (1,))).astype(BF)
        stage.begin(8, 9)
        q_ref, k_ref, v_ref, lse_ref, cos_ref, sin_ref = stage.take(*range(2, 8))

        def unrotate(part, at):
            return (part * cos_ref[at, :] - partner_lanes(part) * sin_ref[at, :]).astype(BF)

        def block(i, carry):
            bias = window_bias(scal_ref, i, rows)
            at = pl.ds(pl.multiple_of(i * QB, QB), QB)
            keys = pl.ds(pl.multiple_of(i * QB, QB), WIN)
            cols = [slice(p * 128, (p + 1) * 128) for p in range(pairs)]
            qs = [stack_heads(q_ref[at, c]) for c in cols]
            dms = [stack_heads(dm_s[at, c]) for c in cols]
            scores = [dot(k_ref[keys, c], one, ((1,), (1,))) + bias for c, one in zip(cols, qs)]
            d_probs = [dot(v_ref[keys, c], one, ((1,), (1,))) for c, one in zip(cols, dms)]
            probs = [jnp.exp(one - lse_ref[i, p]) for p, one in enumerate(scores)]
            dots = [jnp.sum(a * b, axis=0, keepdims=True) for a, b in zip(probs, d_probs)]
            d_scores = [(a * (b - c)).astype(BF) for a, b, c in zip(probs, d_probs, dots)]
            d_values = [dot(a.astype(BF), b, ((1,), (0,))) for a, b in zip(probs, dms)]
            d_keys = [dot(a, b, ((1,), (0,))) for a, b in zip(d_scores, qs)]
            both = [dot(k_ref[keys, c], one, ((0,), (0,))) for c, one in zip(cols, d_scores)]
            for p, c in enumerate(cols):
                dv_acc[keys, c] += d_values[p]
                dk_acc[keys, c] += d_keys[p]
                dq_s[at, c] = unrotate(unstack_columns(both[p]) * HEAD_DIM**-0.5, at)
            return carry

        lax.fori_loop(0, rows // QB, block, 0, unroll=2)
        dk_acc[rows + HALF :, :] += dk_acc[:HALF, :]
        dv_acc[rows + HALF :, :] += dv_acc[:HALF, :]

        def finish(i, carry):
            at = pl.ds(pl.multiple_of(i * HALF, HALF), HALF)
            src = pl.ds(pl.multiple_of(HALF + i * HALF, HALF), HALF)
            for p in range(pairs):
                c = slice(p * 128, (p + 1) * 128)
                dk_s[at, c] = unrotate(dk_acc[src, c], at)
            dv_s[at, :] = dv_acc[src, :].astype(BF)
            return carry

        lax.fori_loop(0, ext // HALF, finish, 0)
        for k in (2, 3, 4):
            stage.send(k)
        norm_ref, mt_ref = stage.take(8, 9)
        low = norm_ref[...]
        me = where_ref[2]
        for j, value in enumerate((dq_s, dk_s, dv_s)):
            grad = dot(low[: value.shape[0]], value[...], ((0,), (0,))).astype(BF)
            for b in range(blocks):
                pieces[b ^ me, :, j * width : (j + 1) * width] = grad[b * height : (b + 1) * height]
        grad = jnp.dot(mt_ref[...], da_ref[...], preferred_element_type=F32).astype(BF)
        for b in range(blocks):
            half, row = divmod(b, blocks // 2)
            pieces[b ^ me, :, 3 * width :] = grad[
                row * height : (row + 1) * height, half * width : (half + 1) * width
            ]
        stage.send(1, source=pieces.at[pl.ds(blocks // 2, blocks // 2)])
        stage.send(0, source=pieces.at[pl.ds(0, blocks // 2)])

    block = ((blocks // 2, height, 4 * width), BF)
    inputs = [by_rows(d_attn), wout, q, k, v, lse, *tables, norm, mixed_t]
    return call(
        body,
        [where, scal],
        inputs,
        [block, block, ((rows, width), BF), ((ext, width), BF), ((ext, width), BF)],
        [((rows + 2 * HALF, width), F32)] * 2
        + [((rows, width), BF), ((blocks, height, 4 * width), BF)],
        "attn_back",
        direct=(0, 1),
    )


def gelu_parts(up_in):
    cdf_part = 0.5 * (1.0 + lax.erf(up_in * 0.7071067811865476))
    gelu_out = up_in * cdf_part
    gelu_slope = cdf_part + up_in * jnp.exp(-0.5 * up_in * up_in) * 0.3989422804014327
    return (gelu_out, gelu_slope)


def together(*values):
    return lax.optimization_barrier(values)


def after(value, *others):
    return lax.optimization_barrier((value, *others))[0]


def pick(index, array, dim=0):
    size = array.shape[dim] // 2
    return lax.dynamic_slice_in_dim(array, index * size, size, dim)


def trade(array, axis):
    flat = array.reshape(-1, array.shape[-1])
    return lax.ppermute(flat, axis, SWAP).reshape(array.shape)


def add(kept, recv):
    return (kept.astype(F32) + recv.astype(F32)).astype(BF)


def add3(one, two, three):
    return (one.astype(F32) + two.astype(F32) + three.astype(F32)).astype(BF)


def adds(kept, recv):
    half = kept.shape[0] // 2
    return add(kept[:half], recv[:half]), add(kept[half:], recv[half:])


def halve(array, bit):
    half = array.shape[0] // 2
    return add(array[:half], flip(array[half:], bit))


def widen(array, bit):
    return jnp.concatenate([array, flip(array, bit)], axis=0)


def split(results):
    return tuple(results[2:]), results[:2]


def flip(array, bit):
    count = lax.axis_size("hi")
    flat = array.reshape(-1, array.shape[-1])
    return lax.ppermute(flat, "hi", [(i, i ^ bit) for i in range(count)]).reshape(array.shape)


def rows_back(where, grads_o, grads_x, w_o, w_x):
    rows, width = grads_o[0].shape
    dim = w_o.shape[1]
    step = rows // CHUNKS

    def body(stage, scalars, outs, scratch):
        dn_ref, halo_ref = outs
        stage.begin(*range(8))
        stage.take(*range(8))
        sides = [stage.buffers[:4], stage.buffers[4:8]]

        def back(at, which):
            total = None
            for w_ref, *grads in sides:
                for j in which:
                    one = dot(grads[j][at, :], w_ref[j], ((1,), (1,)))
                    total = one if total is None else total + one
            return total

        halo_ref[...] = back(slice(rows, rows + HALF), (1, 2))
        stage.send(1)
        for c in range(CHUNKS):
            at = slice(c * step, (c + 1) * step)
            dn_ref[at, :] = back(at, (0, 1, 2))
            stage.send(0, c)

    return call(
        body,
        [where],
        [w_o, *grads_o, w_x, *grads_x],
        [((rows, dim), F32), ((HALF, dim), F32)],
        [],
        "rows_back",
    )


def assemble_ff(where, pieces, ff):
    each, height, dim = pieces[0].shape

    def body(stage, scalars, outs, scratch):
        stage.begin(0, 1, 2, 3)
        (where_ref,) = scalars
        gi_ref, gd_ref = outs
        (whole,) = scratch
        for k in range(4):
            piece = stage.take(k)
            for b in range(each):
                whole[where_ref[2] ^ (k * each + b)] = piece[b]
        for out, index in ((0, 0), (0, 1), (1, 2)):
            row, stop = index * ff, (index + 1) * ff
            while row < stop:
                block, inside = divmod(row, height)
                count = min(height - inside, stop - row)
                part = whole[block, inside : inside + count, :].astype(F32)
                at = slice(row - index * ff, row - index * ff + count)
                if out == 0:
                    gi_ref[index, at, :] = part
                else:
                    gd_ref[at, :] = part
                row += count
        stage.send(0)
        stage.send(1)

    return call(
        body,
        [where],
        list(pieces),
        [((2, ff, dim), F32), ((ff, dim), F32)],
        [((4 * each, height, dim), BF)],
        "assemble_ff",
    )


def assemble_attn(where, pieces, heads):
    count, height, width = pieces[0].shape
    blocks = 4 * count

    def body(stage, scalars, outs, scratch):
        stage.begin(0, 1, 2, 3)
        (where_ref,) = scalars
        gq_ref, go_ref = outs
        (whole,) = scratch
        for k in range(4):
            piece = stage.take(k)
            for b in range(count):
                whole[where_ref[2] ^ (k * count + b)] = piece[b]
        for b in range(blocks):
            at = slice(b * height, (b + 1) * height)
            for j in range(3):
                gq_ref[j, at, :] = whole[b, :, j * heads : (j + 1) * heads].astype(F32)
        stage.send(0)
        for b in range(blocks):
            half, row = divmod(b, blocks // 2)
            go_ref[row * height : (row + 1) * height, half * heads : (half + 1) * heads] = whole[
                b, :, 3 * heads :
            ].astype(F32)
        stage.send(1)

    return call(
        body,
        [where],
        list(pieces),
        [((3, blocks * height, heads), F32), ((heads, 2 * heads), F32)],
        [((blocks, height, width), BF)],
        "assemble_attn",
    )


def per_device(
    tokens_in, seq_lengths, norm1_gain, norm2_gain, w_qkv, w_out, w_in, w_down, out_grad
):
    rows, width = tokens_in.shape
    tensor = lax.axis_index("tensor")
    core = lax.axis_index("core")
    lo = lax.axis_index("lo")
    place = 2 * core + lo
    chips = lax.axis_size("hi")
    hi = lax.axis_index("hi")
    w_in = jnp.swapaxes(w_in, 1, 2)
    me, bit = place, 1
    while bit < chips:
        me, bit = 2 * me + (hi // bit) % 2, 2 * bit
    where = jnp.stack([core, place, me]).astype(jnp.int32)

    edge = jnp.where(tensor == 0, tokens_in[rows - HALF :], tokens_in[:HALF])
    halo = trade(edge, "tensor")
    picked = pick(core, w_qkv, 1)
    halo, picked, where = together(halo, picked, where)
    qkv_across = trade(picked, "tensor")

    lengths = seq_lengths[0]
    own0 = tensor * rows
    halo0 = jnp.where(tensor == 0, rows, rows - HALF)
    scal = jnp.stack([core, lengths[0], lengths[0] + lengths[1], own0, halo0]).astype(jnp.int32)

    q_o, k_o, v_o, mixed_o, lse_o, norm1, *tables = qkv_attn(
        scal, w_qkv, tokens=tokens_in, halo=halo, gain=norm1_gain
    )
    qkv_across, mixed_o = together(after(qkv_across, mixed_o), mixed_o)
    w_qkv_x = (qkv_across, trade(qkv_across, "core"), 1)
    rows_across = jnp.concatenate([pick(core, w_out), pick(core, w_down)], axis=0)
    rows_across = trade(after(rows_across, mixed_o), "tensor")
    q_x, k_x, v_x, mixed_x, lse_x = qkv_attn(
        scal, w_qkv_x, norm=norm1, tables=tables
    )
    in_across = trade(after(pick(core, w_in, 1), mixed_x), "tensor")
    rows_across = after(rows_across, mixed_x)
    rows_beside = trade(rows_across, "core")
    split_at, split_rest = w_out.shape[0] // 2, w_down.shape[0] // 2
    w_out_x = (rows_across, rows_beside, 0, 0, split_at)
    w_down_x = (rows_across, rows_beside, 0, split_at, split_rest)

    ffa_o, ffb_o, norm2, residual, share, dn2 = ffn(
        where, 4 * chips, out_grad, w_in, w_down, norm2_gain,
        start=(tokens_in, mixed_o, mixed_x, w_out, w_out_x),
    )
    share, dn2, ffa_o, ffb_o, in_across = together(
        share, dn2, ffa_o, ffb_o, after(in_across, ffa_o)
    )
    ff_o = adds(ffa_o, trade(ffb_o, "core"))
    w_in_x = (in_across, trade(in_across, "core"), 1)
    ffo_side = trade(ff_o[1], "lo")
    w_in_x = (w_in_x[0], after(w_in_x[1], *ff_o), 1)
    ffa_x, ffb_x, out_tokens, d_res, d_attn, gain_two = ffn(
        where, 4 * chips, out_grad, w_in_x, w_down_x, norm2_gain, carry_in=(norm2, residual, share, dn2)
    )
    out_tokens, d_res, d_attn, gain_two, ffa_x, ffb_x, ffo_side = together(
        out_tokens, d_res, d_attn, gain_two, ffa_x, ffb_x, after(ffo_side, ffa_x)
    )
    ff_o = add(ff_o[0], ffo_side)
    ff_x = adds(ffa_x, trade(ffb_x, "core"))
    ffx_side = trade(ff_x[1], "lo")
    d_attn = after(d_attn, *ff_x, ff_o)

    grads_x, (ata_x, atb_x) = split(
        attn_back(
            scal, where, 4 * chips, (q_x, k_x, v_x, mixed_x, lse_x), d_attn, w_out_x, norm1, tables
        )
    )
    ata_x, atb_x, ffx_side = together(ata_x, atb_x, after(ffx_side, ata_x))
    ff_x = add(ff_x[0], ffx_side)
    ff_recv = trade(ff_x, "tensor")
    at_x = adds(ata_x, trade(atb_x, "core"))
    atx_side = trade(at_x[1], "lo")
    q_o = after(q_o, *at_x, ff_x)
    grads_o, (ata_o, atb_o) = split(
        attn_back(
            scal, where, 4 * chips, (q_o, k_o, v_o, mixed_o, lse_o), d_attn, w_out, norm1, tables
        )
    )
    ata_o, atb_o, atx_side, ff_recv = together(
        ata_o, atb_o, after(atx_side, ata_o), after(ff_recv, ata_o)
    )
    ff_all = adds(ff_o, ff_recv)
    at_x = add(at_x[0], atx_side)
    at_recv = trade(at_x, "tensor")
    at_o = adds(ata_o, trade(atb_o, "core"))
    ato_side = trade(at_o[1], "lo")
    at = add3(at_o[0], ato_side, at_recv)
    dn1, dn1_halo = rows_back(
        where, grads_o, (after(grads_x[0], at), *grads_x[1:]), w_qkv, w_qkv_x
    )
    ff_all, bit = add(ff_all[0], after(flip(ff_all[1], 1), at_x, *at_o)), 2
    while bit < chips:
        ff_all, bit = halve(ff_all, bit), 2 * bit
    while bit > 1:
        bit //= 2
        ff_all = widen(ff_all, bit)

    half = at.shape[0] // 2
    at = add(at[:half], after(flip(at[half:], 1), dn1))
    dn1, dn1_halo = after(dn1, at), after(dn1_halo, at)

    tokens_ext = jnp.concatenate([after(tokens_in, dn1), halo], axis=0).astype(F32)
    normed_one, factor_one = normalize(tokens_ext)
    gain_one = jnp.sum(dn1 * normed_one[:rows], axis=0) + jnp.sum(dn1_halo * normed_one[rows:], axis=0)
    norms = jnp.stack([gain_one, jnp.sum(gain_two, axis=0)])
    back_edge = trade(dn1_halo, "tensor")
    zeros = jnp.zeros((rows - HALF, width), F32)
    d_norm1 = dn1 + jnp.where(
        tensor == 0,
        jnp.concatenate([zeros, back_edge], axis=0),
        jnp.concatenate([back_edge, zeros], axis=0),
    )
    in_grad = (
        d_res + norm_back(d_norm1, norm1_gain, normed_one[:rows], factor_one[:rows])
    ).astype(BF)
    bit = 2
    while bit < chips:
        half = at.shape[0] // 2
        at = add(at[:half], after(flip(at[half:], bit), norms))
        bit *= 2
    everywhere = ("hi", "lo", "core", "tensor")
    spread = jnp.broadcast_to(norms[None], (lax.axis_size(everywhere), 2, width))
    norms = jnp.sum(lax.all_to_all(spread, everywhere, 0, 0), axis=0)

    while bit > 1:
        bit //= 2
        at = widen(at, bit)

    def gather(mine, *others):
        side = after(trade(mine, "lo"), *others)
        return (mine, side, trade(mine, "core"), trade(side, "core"))

    grad_in, grad_down = assemble_ff(where, gather(ff_all), w_in.shape[1])
    grad_in = jnp.swapaxes(grad_in, 1, 2)
    grad_qkv, grad_out = assemble_attn(where, gather(at, grad_down, in_grad, norms), w_qkv.shape[2])

    return (out_tokens, in_grad, norms[0], norms[1], grad_qkv, grad_out, grad_in, grad_down)


def solution(mesh):
    grid = Mesh(mesh.devices.reshape(mesh.shape["dp"] // 4, 2, 2, 2), ("hi", "lo", "core", "tensor"))
    rows = P(("hi", "lo", "core", "tensor"), None)
    weights = (P(None, None, "tensor"), P("tensor", None), P(None, None, "tensor"), P("tensor", None))
    return jax.shard_map(
        per_device,
        mesh=grid,
        in_specs=(rows, P(("hi", "lo", "core"), None), P(), P(), *weights, rows),
        out_specs=(rows, rows, P(), P(), *weights),
        check_vma=False,
    )
```

```python
import jax
import jax.numpy as jnp
import numpy as np
from jax import lax
from jax.experimental import pallas as pl
from jax.experimental.pallas import tpu as pltpu
from jax.sharding import Mesh, PartitionSpec as P

HEAD_DIM = 64
HALF = 64
QB = 128
WIN = QB + 2 * HALF
SWAP = [(0, 1), (1, 0)]
BF = jnp.bfloat16
F32 = jnp.float32


def vmem(megabytes):
    return pltpu.CompilerParams(vmem_limit_bytes=megabytes * 1024 * 1024)


def normalize(values):
    centred = values - jnp.mean(values, axis=-1, keepdims=True)
    factor = lax.rsqrt(jnp.mean(centred * centred, axis=-1, keepdims=True) + 1e-05)
    return (centred * factor, factor)


def norm_back(d_norm, gain_vec, normed, factor):
    scaled = d_norm * gain_vec
    return factor * (
        scaled
        - jnp.mean(scaled, axis=-1, keepdims=True)
        - normed * jnp.mean(scaled * normed, axis=-1, keepdims=True)
    )


def partner_lanes(values):
    lane = lax.broadcasted_iota(jnp.int32, values.shape, 1)
    lower = (lane & 32) == 0
    width = values.shape[1]
    return jnp.where(
        lower, pltpu.roll(values, width - 32, 1), pltpu.roll(values, 32, 1)
    )


def window_bias(scal_ref, block, rows):
    e0, e1, t0, h0 = scal_ref[1], scal_ref[2], scal_ref[3], scal_ref[4]
    j = block * QB + lax.broadcasted_iota(jnp.int32, (WIN, QB), 0)
    t = t0 + block * QB + lax.broadcasted_iota(jnp.int32, (WIN, QB), 1)
    u = jnp.where(
        j < HALF, h0 + j, jnp.where(j >= rows + HALF, h0 + j - rows - HALF, t0 + j - HALF)
    )
    seg_t = (t >= e0).astype(jnp.int32) + (t >= e1).astype(jnp.int32)
    seg_u = (u >= e0).astype(jnp.int32) + (u >= e1).astype(jnp.int32)
    allowed = (seg_t == seg_u) & (jnp.abs(t - u) <= HALF)
    bias = jnp.where(allowed, 0.0, -1e30).astype(F32)
    return jnp.concatenate([bias, bias], axis=1)


def stack_heads(pair):
    lower = lax.broadcasted_iota(jnp.int32, pair.shape, 1) < HEAD_DIM
    zero = jnp.zeros_like(pair)
    return jnp.concatenate(
        [jnp.where(lower, pair, zero), jnp.where(lower, zero, pair)], axis=0
    )


def unstack_columns(both):
    return jnp.concatenate(
        [both[:HEAD_DIM, :QB], both[HEAD_DIM:, QB:]], axis=0
    ).T


def dot(a, b, contract):
    return lax.dot_general(a, b, ((contract[0], contract[1]), ((), ())), preferred_element_type=F32)


CHUNKS = 3


class Stage:
    def __init__(self, copies, buffers, results, out_bufs, out_sems):
        self.copies, self.buffers = copies, buffers
        self.results, self.out_bufs, self.out_sems = results, out_bufs, out_sems
        self.sent = []

    def chosen(self, which):
        for one in which:
            k, chunk = one if isinstance(one, tuple) else (one, None)
            for at, group in enumerate(self.copies[k]):
                if chunk is None or at == chunk:
                    yield from group

    def begin(self, *which):
        for copy in self.chosen(which):
            copy.start()

    def take(self, *which):
        for copy in self.chosen(which):
            copy.wait()
        found = tuple(self.buffers[one[0] if isinstance(one, tuple) else one] for one in which)
        return found if len(found) > 1 else found[0]

    def send(self, k, chunk=None, source=None):
        source = self.out_bufs[k] if source is None else source
        target = self.results[k]
        if chunk is not None:
            rows = target.shape[0] // CHUNKS
            at = pl.ds(chunk * rows, rows)
            source, target = source.at[at], target.at[at]
        copy = pltpu.make_async_copy(source, target, self.out_sems.at[k, chunk or 0])
        copy.start()
        self.sent.append(copy)

    def finish(self):
        for copy in self.sent:
            copy.wait()


def by_rows(array):
    return (array,)


def call(body, scalars, inputs, outs, scratch, name, direct=()):
    flat, shapes, total = [], [], 0
    for one in inputs:
        parts = one if isinstance(one, tuple) else (one,)
        shape = list(parts[0].shape)
        if len(parts) == 5:
            shape[0] = parts[4]
        if len(parts) >= 3:
            shape[parts[2]] *= 2
        flat += list(parts[:2])
        shapes.append(pltpu.VMEM(tuple(shape), parts[0].dtype))
    n_in, n_out, n_scal = len(flat), len(outs), len(scalars)
    buffered = [k for k in range(n_out) if k not in direct]

    def kernel(*refs):
        scal, refs = refs[:n_scal], refs[n_scal:]
        hbm, refs = refs[:n_in], refs[n_in:]
        results, refs = refs[:n_out], refs[n_out:]
        bufs, refs = refs[: len(inputs)], refs[len(inputs) :]
        held = dict(zip(buffered, refs))
        refs = refs[len(buffered) :]
        in_sems, out_sems, refs = refs[0], refs[1], refs[2:]
        copies, at, sem = [], 0, 0
        for one, buffer in zip(inputs, bufs):
            if not isinstance(one, tuple):
                pairs = [[(hbm[at], buffer)]]
                at += 1
            elif len(one) == 1:
                rows = buffer.shape[0] // CHUNKS
                cuts = [pl.ds(c * rows, rows) for c in range(CHUNKS)]
                pairs = [[(hbm[at].at[cut], buffer.at[cut])] for cut in cuts]
                at += 1
            else:
                dim, core = one[2], scal[0][0]
                size = buffer.shape[dim] // 2
                pairs = [[]]
                for ref, index in ((hbm[at], core), (hbm[at + 1], 1 - core)):
                    if len(one) == 5:
                        ref = ref.at[pl.ds(one[3], one[4])]
                    cut = [slice(None)] * len(buffer.shape)
                    cut[dim] = pl.ds(pl.multiple_of(index * size, size), size)
                    pairs[0].append((ref, buffer.at[tuple(cut)]))
                at += 2
            groups = []
            for group in pairs:
                made = []
                for source, target in group:
                    made.append(pltpu.make_async_copy(source, target, in_sems.at[sem]))
                    sem += 1
                groups.append(made)
            copies.append(groups)
        stage = Stage(copies, bufs, results, held, out_sems)
        body(stage, scal, [held.get(k) for k in range(n_out)], refs)
        stage.finish()

    return pl.pallas_call(
        kernel,
        out_shape=tuple(jax.ShapeDtypeStruct(shape, kind) for shape, kind in outs),
        in_specs=[pl.BlockSpec(memory_space=pltpu.SMEM)] * n_scal
        + [pl.BlockSpec(memory_space=pl.ANY)] * n_in,
        out_specs=(pl.BlockSpec(memory_space=pl.ANY),) * n_out,
        scratch_shapes=shapes
        + [pltpu.VMEM(*outs[k]) for k in buffered]
        + [
            pltpu.SemaphoreType.DMA((CHUNKS * len(inputs) + n_in,)),
            pltpu.SemaphoreType.DMA((n_out, CHUNKS)),
        ]
        + [pltpu.VMEM(shape, kind) for shape, kind in scratch],
        compiler_params=vmem(61),
        cost_estimate=pl.CostEstimate(flops=1000, bytes_accessed=1000, transcendentals=0),
        name=name,
    )(*scalars, *flat)


def qkv_attn(scal, w, norm=None, tables=None, tokens=None, halo=None, gain=None):
    first = tokens is not None
    width, dim = (w[0] if isinstance(w, tuple) else w).shape[2], w[0].shape[-2]
    if isinstance(w, tuple):
        dim *= 2
    rows = tokens.shape[0] if first else norm.shape[0] - HALF
    ext = rows + HALF
    pairs = width // 128
    step = 208 if ext % 208 == 0 else 64
    frequency = 10000.0 ** (-np.arange(0, HEAD_DIM, 2, dtype=np.float32) / np.float32(HEAD_DIM))

    def body(stage, scalars, outs, scratch):
        (scal_ref,) = scalars
        q_ref, k_ref, v_ref, mixedt_ref, lse_ref = outs[:5]
        (q_scr,) = scratch
        if first:
            norm_ref, cos_ref, sin_ref = outs[5:]
            stage.begin(0, 1, 2, 3, 4)
            freq_ref, tok_ref, halo_ref, gain_ref = stage.take(0, 1, 2, 3)

            def norm_rows(src_ref, src, dst):
                normed, _ = normalize(src_ref[src, :].astype(F32))
                norm_ref[dst, :] = (normed * gain_ref[...]).astype(BF)

            def norm_step(i, carry):
                at = pl.ds(pl.multiple_of(i * QB, QB), QB)
                norm_rows(tok_ref, at, at)
                return carry

            lax.fori_loop(0, rows // QB, norm_step, 0, unroll=2)
            norm_rows(halo_ref, slice(0, HALF), slice(rows, ext))
            stage.send(5)

            def angles(i, carry):
                at = pl.ds(pl.multiple_of(i * HALF, HALF), HALF)
                j = i * HALF + lax.broadcasted_iota(jnp.int32, (HALF, 128), 0)
                e0, e1 = scal_ref[1], scal_ref[2]
                t = jnp.where(j < rows, scal_ref[3] + j, scal_ref[4] + j - rows)
                opening = jnp.where(t >= e1, e1, jnp.where(t >= e0, e0, 0))
                angle = (t - opening).astype(F32) * freq_ref[...]
                lane = lax.broadcasted_iota(jnp.int32, (HALF, 128), 1)
                sine = jnp.sin(angle)
                cos_ref[at, :] = jnp.cos(angle)
                sin_ref[at, :] = jnp.where((lane & 32) == 0, -sine, sine)
                return carry

            lax.fori_loop(0, ext // HALF, angles, 0, unroll=True)
            stage.send(6)
            stage.send(7)
            w_ref = stage.take(4)
        else:
            stage.begin(0, 1, 2, 3)
            norm_ref, cos_ref, sin_ref, w_ref = stage.take(0, 1, 2, 3)

        def project(i, carry):
            at = pl.ds(pl.multiple_of(i * step, 16), step)
            low = norm_ref[at, :]
            cosine, sine = cos_ref[at, :], sin_ref[at, :]
            raw_q = jnp.dot(low, w_ref[0], preferred_element_type=F32)
            raw_k = jnp.dot(low, w_ref[1], preferred_element_type=F32)
            raw_v = jnp.dot(low, w_ref[2], preferred_element_type=F32)
            out = pl.ds(pl.multiple_of(HALF + i * step, 16), step)
            for p in range(pairs):
                cols = slice(p * 128, (p + 1) * 128)
                part = raw_q[:, cols]
                turned = (part * cosine + partner_lanes(part) * sine).astype(BF)
                q_scr[at, cols] = turned * BF(HEAD_DIM**-0.5)
                part = raw_k[:, cols]
                k_ref[out, cols] = (part * cosine + partner_lanes(part) * sine).astype(BF)
            v_ref[out, :] = raw_v.astype(BF)
            return carry

        lax.fori_loop(0, ext // step, project, 0, unroll=True)
        k_ref[:HALF, :] = k_ref[rows + HALF :, :]
        v_ref[:HALF, :] = v_ref[rows + HALF :, :]
        stage.send(0, source=q_scr.at[pl.ds(0, rows)])
        stage.send(1)
        stage.send(2)

        def block(i, carry):
            bias = window_bias(scal_ref, i, rows)
            at = pl.ds(pl.multiple_of(i * QB, QB), QB)
            keys = pl.ds(pl.multiple_of(i * QB, QB), WIN)
            cols = [slice(p * 128, (p + 1) * 128) for p in range(pairs)]
            scores = [
                dot(k_ref[keys, c], stack_heads(q_scr[at, c]), ((1,), (1,))) + bias for c in cols
            ]
            peaks = [jnp.max(one, axis=0, keepdims=True) for one in scores]
            raws = [jnp.exp(one - peak) for one, peak in zip(scores, peaks)]
            totals = [jnp.sum(one, axis=0, keepdims=True) for one in raws]
            probs = [(one * (1.0 / total)).astype(BF) for one, total in zip(raws, totals)]
            both = [dot(v_ref[keys, c], one, ((0,), (0,))) for c, one in zip(cols, probs)]
            for p, c in enumerate(cols):
                flipped = jnp.concatenate(
                    [both[p][:HEAD_DIM, :QB], both[p][HEAD_DIM:, QB:]], axis=0
                )
                mixedt_ref[c, at] = flipped.astype(BF)
                lse_ref[i, p] = peaks[p] + jnp.log(totals[p])
            return carry

        lax.fori_loop(0, rows // QB, block, 0, unroll=2)
        stage.send(3)
        stage.send(4)

    outs = [
        ((rows, width), BF),
        ((rows + 2 * HALF, width), BF),
        ((rows + 2 * HALF, width), BF),
        ((width, rows), BF),
        ((rows // QB, pairs, 1, 2 * QB), F32),
    ]
    if first:
        outs += [((ext, dim), BF), ((ext, 128), F32), ((ext, 128), F32)]
        inputs = [np.tile(frequency.astype(np.float32), 4).reshape(1, 128), tokens, halo, gain.reshape(1, dim), w]
    else:
        inputs = [norm, *tables, w]
    return call(body, [scal], inputs, outs, [((ext, width), BF)], "qkv_attn", direct=(0,))


def store_rows(pieces, place, start, value):
    size, stop = pieces.shape[1], start + value.shape[0]
    row = start
    while row < stop:
        block, inside = divmod(row, size)
        count = min(size - inside, stop - row)
        part = value[row - start : row - start + count].astype(BF)
        pieces[block ^ place, inside : inside + count, :] = part
        row += count


def ffn(where, blocks, dy, win, wdown, gain, start=None, carry_in=None):
    last = start is None
    rows, dim = dy.shape
    ff = win[0].shape[1] * 2 if isinstance(win, tuple) else win.shape[1]
    height = -(-3 * ff // 256) * 256 // blocks
    step = rows // CHUNKS

    def body(stage, scalars, outs, scratch):
        (where_ref,) = scalars
        act_s, d_s, pieces = scratch[:3]
        if last:
            win_ref, wd_ref, gain_ref, n_ref, dy_ref, res_ref, share_in, dn_in = stage.buffers
            _, _, out_ref, dres_ref, dattn_ref, gn_ref = outs
            gn_ref[...] = jnp.zeros_like(gn_ref)
            stage.begin(0, (3, 0), 1, (4, 0), 2)
            for c in range(CHUNKS):
                if c:
                    stage.begin((3, c), (4, c))
                stage.begin((5, c), (6, c), (7, c))
            stage.take(0, 1, 2)
        else:
            win_ref, wd_ref, gain_ref, wo_ref, wx_ref, mo_ref, mx_ref, tok_ref, dy_ref = stage.buffers
            _, _, n_ref, res_ref, share_ref, dn_ref = outs
            stage.begin(3, 4, 5, 6, (7, 0), 2, 0, 1, (8, 0))
            for c in range(1, CHUNKS):
                stage.begin((7, c), (8, c))
            stage.take(2, 3, 4, 5, 6)

        for c in range(CHUNKS):
            at = slice(c * step, (c + 1) * step)
            if last:
                stage.take((3, c), (4, c))
                low = n_ref[at, :]
            else:
                stage.take((7, c))
                residual = tok_ref[at, :].astype(F32) + (
                    dot(mo_ref[:, at], wo_ref[...], ((0,), (0,)))
                    + dot(mx_ref[:, at], wx_ref[...], ((0,), (0,)))
                )
                res_ref[at, :] = residual
                stage.send(3, c)
                low = (normalize(residual)[0] * gain_ref[...]).astype(BF)
                n_ref[at, :] = low
                stage.send(2, c)
                if c == 0:
                    stage.take(0, 1)
                stage.take((8, c))
            up_in = dot(low, win_ref[0], ((1,), (1,)))
            gate = dot(low, win_ref[1], ((1,), (1,)))
            gelu_out, gelu_slope = gelu_parts(up_in)
            act = (gelu_out * gate).astype(BF)
            act_s[at, :] = act
            share = jnp.dot(act, wd_ref[...], preferred_element_type=F32)
            d_act = dot(dy_ref[at, :], wd_ref[...], ((1,), (1,)))
            d_up = (d_act * gate * gelu_slope).astype(BF)
            d_gate = (d_act * gelu_out).astype(BF)
            d_s[at, :ff] = d_up
            d_s[at, ff:] = d_gate
            dn = jnp.dot(d_up, win_ref[0], preferred_element_type=F32) + jnp.dot(
                d_gate, win_ref[1], preferred_element_type=F32
            )
            if last:
                stage.take((5, c), (6, c), (7, c))
                residual = res_ref[at, :]
                out_ref[at, :] = (residual + (share_in[at, :].astype(F32) + share)).astype(BF)
                stage.send(2, c)
                dn = dn + dn_in[at, :].astype(F32)
                normed, factor = normalize(residual)
                gn_ref[...] += jnp.sum((dn * normed).reshape(step // 8, 8, dim), axis=0)
                d_res = dy_ref[at, :].astype(F32) + norm_back(dn, gain_ref[...], normed, factor)
                dres_ref[at, :] = d_res
                dattn_ref[at, :] = d_res.astype(BF)
                stage.send(3, c)
                stage.send(4, c)
            else:
                share_ref[at, :] = share.astype(BF)
                dn_ref[at, :] = dn.astype(BF)
                stage.send(4, c)
                stage.send(5, c)

        if last:
            stage.send(5)
        place = where_ref[2]
        for c in range(0, 2 * ff, 384):
            value = dot(d_s[:, c : c + 384], n_ref[...], ((0,), (0,)))
            store_rows(pieces, place, c, value)
        store_rows(pieces, place, 2 * ff, dot(act_s[...], dy_ref[...], ((0,), (0,))))
        if blocks * height > 3 * ff:
            store_rows(pieces, place, 3 * ff, jnp.zeros((blocks * height - 3 * ff, dim), F32))
        stage.send(1, source=pieces.at[pl.ds(blocks // 2, blocks // 2)])
        stage.send(0, source=pieces.at[pl.ds(0, blocks // 2)])

    block = ((blocks // 2, height, dim), BF)
    gain = gain.reshape(1, dim)
    if last:
        norm, residual, share, dn = carry_in
        inputs = [win, wdown, gain] + [by_rows(one) for one in (norm, dy, residual, share, dn)]
        outs = [((rows, dim), BF), ((rows, dim), F32), ((rows, dim), BF), ((8, dim), F32)]
    else:
        tokens, mixed_o, mixed_x, wo, wx = start
        inputs = [win, wdown, gain, wo, wx, mixed_o, mixed_x, by_rows(tokens), by_rows(dy)]
        outs = [((rows, dim), BF), ((rows, dim), F32)] + [((rows, dim), BF)] * 2
    return call(
        body,
        [where],
        inputs,
        [block, block, *outs],
        [((rows, ff), BF), ((rows, 2 * ff), BF), ((blocks, height, dim), BF)],
        "ffn",
        direct=(0, 1),
    )


def attn_back(scal, where, blocks, saved, d_attn, wout, norm, tables):
    q, k, v, mixed_t, lse = saved
    rows, width = q.shape
    dim = d_attn.shape[1]
    ext = rows + HALF
    pairs = width // 128
    height = dim // blocks
    step = rows // CHUNKS

    def body(stage, scalars, outs, scratch):
        where_ref, scal_ref = scalars
        dq_s, dk_s, dv_s = outs[2:]
        stage.begin(1, 0, *range(2, 8))
        dk_acc, dv_acc, dm_s, pieces = scratch
        dk_acc[...] = jnp.zeros_like(dk_acc)
        dv_acc[...] = jnp.zeros_like(dv_acc)
        wo_ref = stage.take(1)
        for c in range(CHUNKS):
            da_ref = stage.take((0, c))
            at = slice(c * step, (c + 1) * step)
            dm_s[at, :] = dot(da_ref[at, :], wo_ref[...], ((1,), (1,))).astype(BF)
        stage.begin(8, 9)
        q_ref, k_ref, v_ref, lse_ref, cos_ref, sin_ref = stage.take(*range(2, 8))

        def unrotate(part, at):
            return (part * cos_ref[at, :] - partner_lanes(part) * sin_ref[at, :]).astype(BF)

        def block(i, carry):
            bias = window_bias(scal_ref, i, rows)
            at = pl.ds(pl.multiple_of(i * QB, QB), QB)
            keys = pl.ds(pl.multiple_of(i * QB, QB), WIN)
            cols = [slice(p * 128, (p + 1) * 128) for p in range(pairs)]
            qs = [stack_heads(q_ref[at, c]) for c in cols]
            dms = [stack_heads(dm_s[at, c]) for c in cols]
            scores = [dot(k_ref[keys, c], one, ((1,), (1,))) + bias for c, one in zip(cols, qs)]
            d_probs = [dot(v_ref[keys, c], one, ((1,), (1,))) for c, one in zip(cols, dms)]
            probs = [jnp.exp(one - lse_ref[i, p]) for p, one in enumerate(scores)]
            dots = [jnp.sum(a * b, axis=0, keepdims=True) for a, b in zip(probs, d_probs)]
            d_scores = [(a * (b - c)).astype(BF) for a, b, c in zip(probs, d_probs, dots)]
            d_values = [dot(a.astype(BF), b, ((1,), (0,))) for a, b in zip(probs, dms)]
            d_keys = [dot(a, b, ((1,), (0,))) for a, b in zip(d_scores, qs)]
            both = [dot(k_ref[keys, c], one, ((0,), (0,))) for c, one in zip(cols, d_scores)]
            for p, c in enumerate(cols):
                dv_acc[keys, c] += d_values[p]
                dk_acc[keys, c] += d_keys[p]
                dq_s[at, c] = unrotate(unstack_columns(both[p]) * HEAD_DIM**-0.5, at)
            return carry

        lax.fori_loop(0, rows // QB, block, 0, unroll=2)
        dk_acc[rows + HALF :, :] += dk_acc[:HALF, :]
        dv_acc[rows + HALF :, :] += dv_acc[:HALF, :]

        def finish(i, carry):
            at = pl.ds(pl.multiple_of(i * HALF, HALF), HALF)
            src = pl.ds(pl.multiple_of(HALF + i * HALF, HALF), HALF)
            for p in range(pairs):
                c = slice(p * 128, (p + 1) * 128)
                dk_s[at, c] = unrotate(dk_acc[src, c], at)
            dv_s[at, :] = dv_acc[src, :].astype(BF)
            return carry

        lax.fori_loop(0, ext // HALF, finish, 0)
        for k in (2, 3, 4):
            stage.send(k)
        norm_ref, mt_ref = stage.take(8, 9)
        low = norm_ref[...]
        me = where_ref[2]
        for j, value in enumerate((dq_s, dk_s, dv_s)):
            grad = dot(low[: value.shape[0]], value[...], ((0,), (0,))).astype(BF)
            for b in range(blocks):
                pieces[b ^ me, :, j * width : (j + 1) * width] = grad[b * height : (b + 1) * height]
        grad = jnp.dot(mt_ref[...], da_ref[...], preferred_element_type=F32).astype(BF)
        for b in range(blocks):
            half, row = divmod(b, blocks // 2)
            pieces[b ^ me, :, 3 * width :] = grad[
                row * height : (row + 1) * height, half * width : (half + 1) * width
            ]
        stage.send(1, source=pieces.at[pl.ds(blocks // 2, blocks // 2)])
        stage.send(0, source=pieces.at[pl.ds(0, blocks // 2)])

    block = ((blocks // 2, height, 4 * width), BF)
    inputs = [by_rows(d_attn), wout, q, k, v, lse, *tables, norm, mixed_t]
    return call(
        body,
        [where, scal],
        inputs,
        [block, block, ((rows, width), BF), ((ext, width), BF), ((ext, width), BF)],
        [((rows + 2 * HALF, width), F32)] * 2
        + [((rows, width), BF), ((blocks, height, 4 * width), BF)],
        "attn_back",
        direct=(0, 1),
    )


def gelu_parts(up_in):
    cdf_part = 0.5 * (1.0 + lax.erf(up_in * 0.7071067811865476))
    gelu_out = up_in * cdf_part
    gelu_slope = cdf_part + up_in * jnp.exp(-0.5 * up_in * up_in) * 0.3989422804014327
    return (gelu_out, gelu_slope)


def together(*values):
    return lax.optimization_barrier(values)


def after(value, *others):
    return lax.optimization_barrier((value, *others))[0]


def pick(index, array, dim=0):
    size = array.shape[dim] // 2
    return lax.dynamic_slice_in_dim(array, index * size, size, dim)


def trade(array, axis):
    flat = array.reshape(-1, array.shape[-1])
    return lax.ppermute(flat, axis, SWAP).reshape(array.shape)


def add(kept, recv):
    return (kept.astype(F32) + recv.astype(F32)).astype(BF)


def add3(one, two, three):
    return (one.astype(F32) + two.astype(F32) + three.astype(F32)).astype(BF)


def adds(kept, recv):
    half = kept.shape[0] // 2
    return add(kept[:half], recv[:half]), add(kept[half:], recv[half:])


def halve(array, bit):
    half = array.shape[0] // 2
    return add(array[:half], flip(array[half:], bit))


def widen(array, bit):
    return jnp.concatenate([array, flip(array, bit)], axis=0)


def split(results):
    return tuple(results[2:]), results[:2]


def flip(array, bit):
    count = lax.axis_size("hi")
    flat = array.reshape(-1, array.shape[-1])
    return lax.ppermute(flat, "hi", [(i, i ^ bit) for i in range(count)]).reshape(array.shape)


def rows_back(where, grads_o, grads_x, w_o, w_x):
    rows, width = grads_o[0].shape
    dim = w_o.shape[1]
    step = rows // CHUNKS

    def body(stage, scalars, outs, scratch):
        dn_ref, halo_ref = outs
        stage.begin(*range(8))
        stage.take(*range(8))
        sides = [stage.buffers[:4], stage.buffers[4:8]]

        def back(at, which):
            total = None
            for w_ref, *grads in sides:
                for j in which:
                    one = dot(grads[j][at, :], w_ref[j], ((1,), (1,)))
                    total = one if total is None else total + one
            return total

        halo_ref[...] = back(slice(rows, rows + HALF), (1, 2))
        stage.send(1)
        for c in range(CHUNKS):
            at = slice(c * step, (c + 1) * step)
            dn_ref[at, :] = back(at, (0, 1, 2))
            stage.send(0, c)

    return call(
        body,
        [where],
        [w_o, *grads_o, w_x, *grads_x],
        [((rows, dim), F32), ((HALF, dim), F32)],
        [],
        "rows_back",
    )


def assemble_ff(where, pieces, ff):
    each, height, dim = pieces[0].shape

    def body(stage, scalars, outs, scratch):
        stage.begin(0, 1, 2, 3)
        (where_ref,) = scalars
        gi_ref, gd_ref = outs
        (whole,) = scratch
        for k in range(4):
            piece = stage.take(k)
            for b in range(each):
                whole[where_ref[2] ^ (k * each + b)] = piece[b]
        for out, index in ((0, 0), (0, 1), (1, 2)):
            row, stop = index * ff, (index + 1) * ff
            while row < stop:
                block, inside = divmod(row, height)
                count = min(height - inside, stop - row)
                part = whole[block, inside : inside + count, :].astype(F32)
                at = slice(row - index * ff, row - index * ff + count)
                if out == 0:
                    gi_ref[index, at, :] = part
                else:
                    gd_ref[at, :] = part
                row += count
        stage.send(0)
        stage.send(1)

    return call(
        body,
        [where],
        list(pieces),
        [((2, ff, dim), F32), ((ff, dim), F32)],
        [((4 * each, height, dim), BF)],
        "assemble_ff",
    )


def assemble_attn(where, pieces, heads):
    count, height, width = pieces[0].shape
    blocks = 4 * count

    def body(stage, scalars, outs, scratch):
        stage.begin(0, 1, 2, 3)
        (where_ref,) = scalars
        gq_ref, go_ref = outs
        (whole,) = scratch
        for k in range(4):
            piece = stage.take(k)
            for b in range(count):
                whole[where_ref[2] ^ (k * count + b)] = piece[b]
        for b in range(blocks):
            at = slice(b * height, (b + 1) * height)
            for j in range(3):
                gq_ref[j, at, :] = whole[b, :, j * heads : (j + 1) * heads].astype(F32)
        stage.send(0)
        for b in range(blocks):
            half, row = divmod(b, blocks // 2)
            go_ref[row * height : (row + 1) * height, half * heads : (half + 1) * heads] = whole[
                b, :, 3 * heads :
            ].astype(F32)
        stage.send(1)

    return call(
        body,
        [where],
        list(pieces),
        [((3, blocks * height, heads), F32), ((heads, 2 * heads), F32)],
        [((blocks, height, width), BF)],
        "assemble_attn",
    )


def per_device(
    tokens_in, seq_lengths, norm1_gain, norm2_gain, w_qkv, w_out, w_in, w_down, out_grad
):
    rows, width = tokens_in.shape
    tensor = lax.axis_index("tensor")
    core = lax.axis_index("core")
    lo = lax.axis_index("lo")
    place = 2 * core + lo
    chips = lax.axis_size("hi")
    hi = lax.axis_index("hi")
    w_in = jnp.swapaxes(w_in, 1, 2)
    me, bit = place, 1
    while bit < chips:
        me, bit = 2 * me + (hi // bit) % 2, 2 * bit
    where = jnp.stack([core, place, me]).astype(jnp.int32)

    edge = jnp.where(tensor == 0, tokens_in[rows - HALF :], tokens_in[:HALF])
    halo = trade(edge, "tensor")
    picked = pick(core, w_qkv, 1)
    halo, picked, where = together(halo, picked, where)
    qkv_across = trade(picked, "tensor")

    lengths = seq_lengths[0]
    own0 = tensor * rows
    halo0 = jnp.where(tensor == 0, rows, rows - HALF)
    scal = jnp.stack([core, lengths[0], lengths[0] + lengths[1], own0, halo0]).astype(jnp.int32)

    q_o, k_o, v_o, mixed_o, lse_o, norm1, *tables = qkv_attn(
        scal, w_qkv, tokens=tokens_in, halo=halo, gain=norm1_gain
    )
    rows_across = after(jnp.concatenate([pick(core, w_out), pick(core, w_down)], axis=0), mixed_o)
    qkv_across, mixed_o, rows_across = together(after(qkv_across, mixed_o), mixed_o, rows_across)
    w_qkv_x = (qkv_across, trade(qkv_across, "core"), 1)
    rows_across = trade(rows_across, "tensor")
    q_x, k_x, v_x, mixed_x, lse_x = qkv_attn(
        scal, w_qkv_x, norm=norm1, tables=tables
    )
    in_across = trade(after(pick(core, w_in, 1), mixed_x), "tensor")
    rows_across = after(rows_across, mixed_x)
    rows_beside = trade(rows_across, "core")
    split_at, split_rest = w_out.shape[0] // 2, w_down.shape[0] // 2
    w_out_x = (rows_across, rows_beside, 0, 0, split_at)
    w_down_x = (rows_across, rows_beside, 0, split_at, split_rest)

    ffa_o, ffb_o, norm2, residual, share, dn2 = ffn(
        where, 4 * chips, out_grad, w_in, w_down, norm2_gain,
        start=(tokens_in, mixed_o, mixed_x, w_out, w_out_x),
    )
    share, dn2, ffa_o, ffb_o, in_across = together(
        share, dn2, ffa_o, ffb_o, after(in_across, ffa_o)
    )
    ff_o = adds(ffa_o, trade(ffb_o, "core"))
    w_in_x = (in_across, trade(in_across, "core"), 1)
    ffo_side = trade(ff_o[1], "lo")
    w_in_x = (w_in_x[0], after(w_in_x[1], *ff_o), 1)
    ffa_x, ffb_x, out_tokens, d_res, d_attn, gain_two = ffn(
        where, 4 * chips, out_grad, w_in_x, w_down_x, norm2_gain, carry_in=(norm2, residual, share, dn2)
    )
    out_tokens, d_res, d_attn, gain_two, ffa_x, ffb_x, ffo_side = together(
        out_tokens, d_res, d_attn, gain_two, ffa_x, ffb_x, after(ffo_side, ffa_x)
    )
    ff_o = add(ff_o[0], ffo_side)
    ff_x = adds(ffa_x, trade(ffb_x, "core"))
    ffx_side = trade(ff_x[1], "lo")
    d_attn = after(d_attn, *ff_x, ff_o)

    grads_x, (ata_x, atb_x) = split(
        attn_back(
            scal, where, 4 * chips, (q_x, k_x, v_x, mixed_x, lse_x), d_attn, w_out_x, norm1, tables
        )
    )
    ata_x, atb_x, ffx_side = together(ata_x, atb_x, after(ffx_side, ata_x))
    ff_x = add(ff_x[0], ffx_side)
    ff_recv = trade(ff_x, "tensor")
    at_x = adds(ata_x, trade(atb_x, "core"))
    atx_side = trade(at_x[1], "lo")
    q_o = after(q_o, *at_x, ff_x)
    grads_o, (ata_o, atb_o) = split(
        attn_back(
            scal, where, 4 * chips, (q_o, k_o, v_o, mixed_o, lse_o), d_attn, w_out, norm1, tables
        )
    )
    ata_o, atb_o, atx_side, ff_recv = together(
        ata_o, atb_o, after(atx_side, ata_o), after(ff_recv, ata_o)
    )
    ff_all = adds(ff_o, ff_recv)
    at_x = add(at_x[0], atx_side)
    at_recv = trade(at_x, "tensor")
    at_o = adds(ata_o, trade(atb_o, "core"))
    ato_side = trade(at_o[1], "lo")
    at = add3(at_o[0], ato_side, at_recv)
    dn1, dn1_halo = rows_back(
        where, grads_o, (after(grads_x[0], at), *grads_x[1:]), w_qkv, w_qkv_x
    )
    ff_all, bit = add(ff_all[0], after(flip(ff_all[1], 1), at_x, *at_o)), 2
    while bit < chips:
        ff_all, bit = halve(ff_all, bit), 2 * bit
    while bit > 1:
        bit //= 2
        ff_all = widen(ff_all, bit)

    half = at.shape[0] // 2
    at = add(at[:half], after(flip(at[half:], 1), dn1))
    dn1, dn1_halo = after(dn1, at), after(dn1_halo, at)

    tokens_ext = jnp.concatenate([after(tokens_in, dn1), halo], axis=0).astype(F32)
    normed_one, factor_one = normalize(tokens_ext)
    gain_one = jnp.sum(dn1 * normed_one[:rows], axis=0) + jnp.sum(dn1_halo * normed_one[rows:], axis=0)
    norms = jnp.stack([gain_one, jnp.sum(gain_two, axis=0)])
    back_edge = trade(dn1_halo, "tensor")
    zeros = jnp.zeros((rows - HALF, width), F32)
    d_norm1 = dn1 + jnp.where(
        tensor == 0,
        jnp.concatenate([zeros, back_edge], axis=0),
        jnp.concatenate([back_edge, zeros], axis=0),
    )
    in_grad = (
        d_res + norm_back(d_norm1, norm1_gain, normed_one[:rows], factor_one[:rows])
    ).astype(BF)
    bit = 2
    while bit < chips:
        half = at.shape[0] // 2
        at = add(at[:half], after(flip(at[half:], bit), norms))
        bit *= 2
    everywhere = ("hi", "lo", "core", "tensor")
    spread = jnp.broadcast_to(norms[None], (lax.axis_size(everywhere), 2, width))
    norms = jnp.sum(lax.all_to_all(spread, everywhere, 0, 0), axis=0)

    while bit > 1:
        bit //= 2
        at = widen(at, bit)

    def gather(mine, *others):
        side = after(trade(mine, "lo"), *others)
        return (mine, side, trade(mine, "core"), trade(side, "core"))

    grad_in, grad_down = assemble_ff(where, gather(ff_all), w_in.shape[1])
    grad_in = jnp.swapaxes(grad_in, 1, 2)
    grad_qkv, grad_out = assemble_attn(where, gather(at, grad_down, in_grad, norms), w_qkv.shape[2])

    return (out_tokens, in_grad, norms[0], norms[1], grad_qkv, grad_out, grad_in, grad_down)


def solution(mesh):
    grid = Mesh(mesh.devices.reshape(mesh.shape["dp"] // 4, 2, 2, 2), ("hi", "lo", "core", "tensor"))
    rows = P(("hi", "lo", "core", "tensor"), None)
    weights = (P(None, None, "tensor"), P("tensor", None), P(None, None, "tensor"), P("tensor", None))
    return jax.shard_map(
        per_device,
        mesh=grid,
        in_specs=(rows, P(("hi", "lo", "core"), None), P(), P(), *weights, rows),
        out_specs=(rows, rows, P(), P(), *weights),
        check_vma=False,
    )
```
